512 devices in a mesh: img: 16 (over y, core), view: 32 (over z, x).
Axes of the slice: x: 4, y: 8, z: 8, core: 2. Of those that a mesh axis runs over, the one named last changes fastest.
Arguments:
- centers: float32 [3, 65536], P(None, ('img', 'view')), may hold values from -1 to 1
- log_scales: float32 [3, 65536], P(None, ('img', 'view')), may hold values from -3 to 0.9
- quaternions: float32 [4, 65536], P(None, ('img', 'view')), may hold values from 0.5 to 1.5
- logits: float32 [65536], P(('img', 'view')), may hold values from -6 to -3
- harmonics: float32 [48, 65536], P(None, ('img', 'view')), may hold values from -3 to 3
- cameras: float32 [32, 3], replicated, may hold values from -3.140625 to 3.140625
- tile_lists: int32 [32, 16, 4, 256], P('view', 'img'), may hold values from 0 to 2047
- tile_counts: int32 [32, 16, 4], P('view', 'img'), may hold values from 1 to 256, as said below
- tile_ids: int32 [32, 16, 4], P('view', 'img'), may hold values from 0 to 63, as said below
- send_index: int32 [32, 16, 16, 128], P('view', 'img'), may hold values from 0 to 4095
- pixel_grad: float32 [32, 16, 4, 3, 256], P('view', 'img'), may hold values from -6 to 6
Outputs:
- rendered: float32 [32, 16, 4, 3, 256], P('view', 'img')
- grad_centers: float32 [3, 65536], P(None, ('img', 'view'))
- grad_scales: float32 [3, 65536], P(None, ('img', 'view'))
- grad_quaternions: float32 [4, 65536], P(None, ('img', 'view'))
- grad_logits: float32 [65536], P(('img', 'view'))
- grad_harmonics: float32 [48, 65536], P(None, ('img', 'view'))
The draws below stay inside these ranges and needn't reach their ends.
Inputs may be any that keep to these rules, and one draw needn't show every extreme that they name: `tile_counts`: each owner of each camera has at least one tile whose count is 256. `tile_ids`: for each camera the tile numbers of all owners together are 0 to 63, each once.
All inputs are finite; a program needn't handle non-finite values.
Results may differ from the reference program's by a relative error of at most 0.0003.
Values sent between devices are 32-bit elements; how exact they have to be, the bound alone decides.
A program may use at most 64 MiB of HBM per device.

```python
import jax
import jax.numpy as jnp
from jax import lax

CAP = 128
LIST = 256
TD = 4
TW = 8
G_IMG = 4096
GAUSSIANS = 65536
TILES = 64
N_IMG = 16
N_VIEW = 32


def draw_tile_counts(key, part):
    key = jax.random.fold_in(key, 11)
    first_key, second_key = jax.random.split(key)
    counts = jax.random.randint(first_key, (N_VIEW, N_IMG, TD), 1, LIST + 1)
    full_slot = jax.random.randint(second_key, (N_VIEW, N_IMG, 1), 0, TD)
    positions = jnp.arange(TD)[None, None, :]
    return jnp.where(positions == full_slot, LIST, counts).astype(jnp.int32)


def draw_tile_ids(key, part):
    key = jax.random.fold_in(key, 23)
    camera_keys = jax.random.split(key, N_VIEW)
    orders = jax.vmap(lambda single: jax.random.permutation(single, TILES))(camera_keys)
    return orders.reshape(N_VIEW, N_IMG, TD).astype(jnp.int32)


def set_ends(values, own_key, low, largest):
    longest = values.shape.index(max(values.shape))
    spots = []
    for shift in (0, 1):
        where = [jax.random.randint(jax.random.fold_in(own_key, axis), (), 0, length) for axis, length in enumerate(values.shape)]
        where[longest] = (where[longest] + shift) % values.shape[longest]
        spots.append(tuple(where))
    return values.at[spots[0]].set(low).at[spots[1]].set(largest)


def block_scale(rng, extent, shards, low, top_value):
    def one(axis_at, blocks):
        draws = jax.random.uniform(jax.random.fold_in(jax.random.fold_in(rng, 6), axis_at), (blocks,), jnp.float32, low / len(shards), top_value / len(shards))
        return jnp.repeat(jnp.exp(draws), extent[axis_at] // blocks).reshape((-1,) + (1,) * (len(extent) - axis_at - 1))

    level = one(*shards[0])
    for cut in shards[1:]:
        level = level * one(*cut)
    return level


def bell_draw(rng, extent, deviation, bound, cuts=(), kind=jnp.bfloat16):
    array = deviation * jax.random.normal(rng, extent, jnp.float32)
    if cuts:
        array = array * block_scale(rng, extent, cuts, -0.22, 0.18)
    return jnp.clip(array, -bound, bound).astype(kind)


def setup_inputs(seed: int = 0) -> dict:
    arg_keys = jax.random.split(jax.random.key(seed), 12)
    centers = jnp.clip(jax.random.uniform(arg_keys[0], (3, GAUSSIANS), jnp.float32, -1.0, 1.0) * block_scale(arg_keys[0], (3, GAUSSIANS), ((1, 512),), -0.4, 0.0), -1.0, 1.0)
    log_scales = jnp.clip(-3.0 + 3.9 * jax.random.uniform(arg_keys[1], (3, GAUSSIANS), jnp.float32) ** block_scale(arg_keys[1], (3, GAUSSIANS), ((1, 512),), -0.2, 0.2), -3.0, 0.9)
    quaternions = jnp.clip(0.5 + 1.0 * jax.random.uniform(arg_keys[2], (4, GAUSSIANS), jnp.float32) ** block_scale(arg_keys[2], (4, GAUSSIANS), ((1, 512),), -0.2, 0.2), 0.5, 1.5)
    logits = jnp.clip(-6.0 + 3.0 * jax.random.uniform(arg_keys[3], (GAUSSIANS,), jnp.float32) ** block_scale(arg_keys[3], (GAUSSIANS,), ((0, 512),), -0.2, 0.2), -6.0, -3.0)
    harmonics = bell_draw(arg_keys[4], (48, GAUSSIANS), 0.5, 3.0, ((1, 512),), jnp.float32)
    cameras = jnp.clip(jax.random.uniform(arg_keys[5], (N_VIEW, 3), jnp.float32, -3.140625, 3.140625), -3.140625, 3.140625)
    tile_lists = set_ends(jax.random.randint(arg_keys[6], (N_VIEW, N_IMG, TD, LIST), 0, N_IMG * CAP), jax.random.fold_in(arg_keys[6], 1), 0, (N_IMG * CAP) - 1).astype(jnp.int32)
    tile_counts = draw_tile_counts(jax.random.fold_in(arg_keys[11], 71), 0)
    tile_ids = draw_tile_ids(jax.random.fold_in(arg_keys[11], 71), 0)
    send_index = set_ends(jax.random.randint(arg_keys[9], (N_VIEW, N_IMG, N_IMG, CAP), 0, G_IMG), jax.random.fold_in(arg_keys[9], 1), 0, G_IMG - 1).astype(jnp.int32)
    pixel_grad = bell_draw(arg_keys[10], (N_VIEW, N_IMG, TD, 3, 256), 1.0, 6.0, ((0, 32), (1, 16)), jnp.float32)
    return dict(centers=centers, log_scales=log_scales, quaternions=quaternions, logits=logits, harmonics=harmonics, cameras=cameras, tile_lists=tile_lists, tile_counts=tile_counts, tile_ids=tile_ids, send_index=send_index, pixel_grad=pixel_grad)


CAMERA_DISTANCE = 4.0
HARMONIC_ZERO = 0.28209479177387814
HARMONIC_ONE = 0.4886025119029199
HARMONIC_TWO = [1.0925484305920792, -1.0925484305920792, 0.31539156525252005, -1.0925484305920792, 0.5462742152960396]
HARMONIC_THREE = [-0.5900435899266435, 2.890611442640554, -0.4570457994644658, 0.3731763325901154, -0.4570457994644658, 1.445305721320277, -0.5900435899266435]

def times_three(left, right):
    return [[left[r][0] * right[0][c] + left[r][1] * right[1][c] + left[r][2] * right[2][c] for c in range(3)] for r in range(3)]

def rotation_matrix(angles):
    cos_a, sin_a = (jnp.cos(angles[0]), jnp.sin(angles[0]))
    cos_b, sin_b = (jnp.cos(angles[1]), jnp.sin(angles[1]))
    cos_g, sin_g = (jnp.cos(angles[2]), jnp.sin(angles[2]))
    about_x = [[1.0, 0.0, 0.0], [0.0, cos_b, -sin_b], [0.0, sin_b, cos_b]]
    about_y = [[cos_a, 0.0, sin_a], [0.0, 1.0, 0.0], [-sin_a, 0.0, cos_a]]
    about_z = [[cos_g, -sin_g, 0.0], [sin_g, cos_g, 0.0], [0.0, 0.0, 1.0]]
    return times_three(about_z, times_three(about_y, about_x))

def project(centers, log_scales, quaternions, logits, harmonics, angles, focal_len, half_w, half_h):
    rotation = rotation_matrix(angles)
    camera = [rotation[r][0] * centers[0] + rotation[r][1] * centers[1] + rotation[r][2] * centers[2] for r in range(3)]
    inv_depth = 1.0 / (camera[2] + CAMERA_DISTANCE)
    screen_u = focal_len * camera[0] * inv_depth + half_w
    screen_v = focal_len * camera[1] * inv_depth + half_h
    unit_q = quaternions / jnp.sqrt(lax.optimization_barrier(jnp.sum(quaternions * quaternions, axis=0)))
    w, x, y, z = (unit_q[0], unit_q[1], unit_q[2], unit_q[3])
    quat_rot = [[1.0 - 2.0 * (y * y + z * z), 2.0 * (x * y - w * z), 2.0 * (x * z + w * y)], [2.0 * (x * y + w * z), 1.0 - 2.0 * (x * x + z * z), 2.0 * (y * z - w * x)], [2.0 * (x * z - w * y), 2.0 * (y * z + w * x), 1.0 - 2.0 * (x * x + y * y)]]
    stretch = jnp.exp(log_scales)
    factor = [[quat_rot[r][c] * stretch[c] for c in range(3)] for r in range(3)]
    jacobian = [[focal_len * inv_depth, 0.0, -focal_len * camera[0] * inv_depth * inv_depth], [0.0, focal_len * inv_depth, -focal_len * camera[1] * inv_depth * inv_depth]]
    to_screen = [[jacobian[a][0] * rotation[0][c] + jacobian[a][1] * rotation[1][c] + jacobian[a][2] * rotation[2][c] for c in range(3)] for a in range(2)]
    screen_factor = [[to_screen[a][0] * factor[0][k] + to_screen[a][1] * factor[1][k] + to_screen[a][2] * factor[2][k] for k in range(3)] for a in range(2)]
    cov = [[screen_factor[a][0] * screen_factor[b][0] + screen_factor[a][1] * screen_factor[b][1] + screen_factor[a][2] * screen_factor[b][2] for b in range(2)] for a in range(2)]
    cov_a = cov[0][0] + 0.3
    cov_b = cov[0][1]
    cov_c = cov[1][1] + 0.3
    determinant = cov_a * cov_c - cov_b * cov_b
    offsets = [centers[c] + CAMERA_DISTANCE * rotation[2][c] for c in range(3)]
    length = jnp.sqrt(offsets[0] * offsets[0] + offsets[1] * offsets[1] + offsets[2] * offsets[2])
    x, y, z = (offsets[0] / length, offsets[1] / length, offsets[2] / length)
    xx, yy, zz = (x * x, y * y, z * z)
    sh_basis = jnp.stack([HARMONIC_ZERO * jnp.ones_like(x), -HARMONIC_ONE * y, HARMONIC_ONE * z, -HARMONIC_ONE * x, HARMONIC_TWO[0] * x * y, HARMONIC_TWO[1] * y * z, HARMONIC_TWO[2] * (2.0 * zz - xx - yy), HARMONIC_TWO[3] * x * z, HARMONIC_TWO[4] * (xx - yy), HARMONIC_THREE[0] * y * (3.0 * xx - yy), HARMONIC_THREE[1] * x * y * z, HARMONIC_THREE[2] * y * (4.0 * zz - xx - yy), HARMONIC_THREE[3] * z * (2.0 * zz - 3.0 * xx - 3.0 * yy), HARMONIC_THREE[4] * x * (4.0 * zz - xx - yy), HARMONIC_THREE[5] * z * (xx - yy), HARMONIC_THREE[6] * x * (xx - 3.0 * yy)])
    colour = jnp.maximum(lax.optimization_barrier(jnp.sum(sh_basis[:, None, :] * harmonics.reshape(16, 3, -1), axis=0)) + 0.5, 0.0)
    opacity = jax.nn.sigmoid(logits)
    geometry = jnp.stack([screen_u, screen_v, cov_c / determinant, -cov_b / determinant, cov_a / determinant])
    return jnp.concatenate([geometry, colour, opacity[None, :]], axis=0)

def blend(proj_rows, tile_list, counts, tile_num, across):
    entries = jnp.take(proj_rows, tile_list, axis=1)
    length = tile_list.shape[1]
    pixel = jnp.arange(256)
    local_x = (pixel % 16).astype(jnp.float32) + 0.5
    local_y = (pixel // 16).astype(jnp.float32) + 0.5
    pix_x = (16 * (tile_num % across)).astype(jnp.float32)[:, None] + local_x[None, :]
    pix_y = (16 * (tile_num // across)).astype(jnp.float32)[:, None] + local_y[None, :]
    diff_x = pix_x[:, :, None] - entries[0][:, None, :]
    diff_y = pix_y[:, :, None] - entries[1][:, None, :]
    exponent = -0.5 * (entries[2][:, None, :] * diff_x * diff_x + 2.0 * entries[3][:, None, :] * diff_x * diff_y + entries[4][:, None, :] * diff_y * diff_y)
    live_mask = (jnp.arange(length)[None, :] < counts[:, None]).astype(jnp.float32)
    alphas = (entries[8] * live_mask)[:, None, :] * jnp.exp(exponent)
    triangle = (jnp.arange(length)[:, None] < jnp.arange(length)[None, :]).astype(jnp.float32)
    log_trans = jnp.einsum('tpk,kj->tpj', jnp.log1p(-alphas), triangle, precision=lax.Precision.HIGHEST)
    weights = alphas * jnp.exp(log_trans)
    return jnp.einsum('tpk,ctk->tcp', weights, entries[5:8], precision=lax.Precision.HIGHEST)

def reference(centers, log_scales, quaternions, logits, harmonics, cameras, tile_lists, tile_counts, tile_ids, send_index, pixel_grad):
    focal_len = 16.0 * TW
    half_w = 8.0 * TW
    half_h = 8.0 * (TILES // TW)
    params = (centers, log_scales, quaternions, logits, harmonics)

    def one_camera(totals, inputs):
        angles, tile_list, counts, tile_num, send_slots, cotangent = inputs
        offset_base = (jnp.arange(N_IMG) * G_IMG).astype(jnp.int32)[:, None, None]
        global_idx = jnp.transpose(send_slots + offset_base, (1, 0, 2)).reshape(N_IMG, N_IMG * CAP)
        entry_idx = jax.vmap(lambda lookup_row, chosen: lookup_row[chosen])(global_idx, tile_list).reshape(N_IMG * TD, LIST)

        def render(*values):
            proj_rows = project(*values, angles, focal_len, half_w, half_h)
            return blend(proj_rows, entry_idx, counts.reshape(-1), tile_num.reshape(-1), TW)
        rendered, pullback = jax.vjp(render, *params)
        increment = pullback(cotangent.reshape(N_IMG * TD, 3, 256))
        totals = tuple((total + extra for total, extra in zip(totals, increment)))
        return (totals, rendered.reshape(N_IMG, TD, 3, 256))
    initial = tuple((jnp.zeros(value.shape, jnp.float32) for value in params))
    totals, rendered = lax.scan(one_camera, initial, (cameras, tile_lists, tile_counts, tile_ids, send_index, pixel_grad))
    return (rendered, totals[0], totals[1], totals[2], totals[3], totals[4])
```

```python
import functools

import jax
import jax.numpy as jnp
from jax import lax
from jax.experimental import pallas as pl
from jax.experimental.pallas import tpu as pltpu
from jax.sharding import PartitionSpec as P

TW = 8
ROWS = 9
LANES = 128
PIX = 256
FINE_ROWS = (2, 3, 4)
LOG2E = 1.4426950408889634
CAMERA_DISTANCE = 4.0
C0 = 0.28209479177387814
C1 = 0.4886025119029199
C20, C21, C22, C23, C24 = (
    1.0925484305920792,
    -1.0925484305920792,
    0.31539156525252005,
    -1.0925484305920792,
    0.5462742152960396,
)
C30, C31, C32, C33, C34, C35, C36 = (
    -0.5900435899266435,
    2.890611442640554,
    -0.4570457994644658,
    0.3731763325901154,
    -0.4570457994644658,
    1.445305721320277,
    -0.5900435899266435,
)
F32 = jnp.float32
BF16 = jnp.bfloat16


def split_two(value):
    high = value.astype(BF16)
    low = (value - high.astype(F32)).astype(BF16)
    return high, low


def dot(left, right):
    return lax.dot_general(left, right, (((1,), (0,)), ((), ())), preferred_element_type=F32)


def dot_nt(left, right):
    return lax.dot_general(left, right, (((1,), (1,)), ((), ())), preferred_element_type=F32)


def rotations(cameras, count):
    cosines, sines = jnp.cos(cameras), jnp.sin(cameras)

    def column(values, k):
        return jnp.broadcast_to(values[:, k : k + 1], (count, LANES))

    ca, cb, cg = (column(cosines, k) for k in range(3))
    sa, sb, sg = (column(sines, k) for k in range(3))
    return [
        [cg * ca, cg * sa * sb - sg * cb, cg * sa * cb + sg * sb],
        [sg * ca, sg * sa * sb + cg * cb, sg * sa * cb - cg * sb],
        [-sa, ca * sb, ca * cb],
    ]


def shape_factor(quats, scales):
    inv = lax.rsqrt(sum(q * q for q in quats))
    w, x, y, z = (q * inv for q in quats)
    rot = [
        [1.0 - 2.0 * (y * y + z * z), 2.0 * (x * y - w * z), 2.0 * (x * z + w * y)],
        [2.0 * (x * y + w * z), 1.0 - 2.0 * (x * x + z * z), 2.0 * (y * z - w * x)],
        [2.0 * (x * z - w * y), 2.0 * (y * z + w * x), 1.0 - 2.0 * (x * x + y * y)],
    ]
    stretch = [jnp.exp(s) for s in scales]
    factor = [[rot[r][k] * stretch[k] for k in range(3)] for r in range(3)]
    return (w, x, y, z), inv, stretch, factor


def basis_of(x, y, z):
    xx, yy, zz = x * x, y * y, z * z
    return [
        None,
        -C1 * y,
        C1 * z,
        -C1 * x,
        C20 * x * y,
        C21 * y * z,
        C22 * (2.0 * zz - xx - yy),
        C23 * x * z,
        C24 * (xx - yy),
        C30 * y * (3.0 * xx - yy),
        C31 * x * y * z,
        C32 * y * (4.0 * zz - xx - yy),
        C33 * z * (2.0 * zz - 3.0 * xx - 3.0 * yy),
        C34 * x * (4.0 * zz - xx - yy),
        C35 * z * (xx - yy),
        C36 * x * (xx - 3.0 * yy),
    ]


def project(rot, centers, factor, harm_ref, focal, half_w, half_h):
    pts = [rot[r][0] * centers[0] + rot[r][1] * centers[1] + rot[r][2] * centers[2] for r in range(3)]
    iz = 1.0 / (pts[2] + CAMERA_DISTANCE)
    fiz = focal * iz
    tx, ty = pts[0] * iz, pts[1] * iz
    t0 = [fiz * (rot[0][c] - tx * rot[2][c]) for c in range(3)]
    t1 = [fiz * (rot[1][c] - ty * rot[2][c]) for c in range(3)]
    s0 = [t0[0] * factor[0][k] + t0[1] * factor[1][k] + t0[2] * factor[2][k] for k in range(3)]
    s1 = [t1[0] * factor[0][k] + t1[1] * factor[1][k] + t1[2] * factor[2][k] for k in range(3)]
    cov_a = s0[0] * s0[0] + s0[1] * s0[1] + s0[2] * s0[2] + 0.3
    cov_b = s0[0] * s1[0] + s0[1] * s1[1] + s0[2] * s1[2]
    cov_c = s1[0] * s1[0] + s1[1] * s1[1] + s1[2] * s1[2] + 0.3
    inv_det = 1.0 / (cov_a * cov_c - cov_b * cov_b)
    conic = (cov_c * inv_det, -cov_b * inv_det, cov_a * inv_det)
    offs = [centers[c] + CAMERA_DISTANCE * rot[2][c] for c in range(3)]
    inv_len = lax.rsqrt(offs[0] * offs[0] + offs[1] * offs[1] + offs[2] * offs[2])
    x, y, z = (o * inv_len for o in offs)
    basis = basis_of(x, y, z)
    shade = []
    for ch in range(3):
        total = 0.5 + C0 * harm_ref[ch : ch + 1, :]
        for l in range(1, 16):
            total = total + basis[l] * harm_ref[3 * l + ch : 3 * l + ch + 1, :]
        shade.append(total)
    colour = [jnp.maximum(s, 0.0) for s in shade]
    values = [focal * tx + half_w, focal * ty + half_h, *conic, *colour]
    saved = (iz, fiz, tx, ty, t0, t1, s0, s1, conic, inv_det, inv_len, (x, y, z), basis, shade)
    return values, saved


def over_cameras(value):
    return jnp.sum(value, axis=0, keepdims=True)


def project_back(rot, factor, harm_ref, focal, saved, grads, grad_harm_ref):
    iz, fiz, tx, ty, t0, t1, s0, s1, conic, inv_det, inv_len, (x, y, z), basis, shade = saved
    du, dv, dca, dcb, dcc = grads[:5]
    dcol = []
    for ch in range(3):
        g = grads[5 + ch]
        dcol.append(jnp.where(shade[ch] > 0.0, g, jnp.where(shade[ch] == 0.0, 0.5 * g, 0.0)))
    e = [None]
    for ch in range(3):
        grad_harm_ref[ch : ch + 1, :] = C0 * over_cameras(dcol[ch])
    for l in range(1, 16):
        e.append(sum(harm_ref[3 * l + ch : 3 * l + ch + 1, :] * dcol[ch] for ch in range(3)))
        for ch in range(3):
            grad_harm_ref[3 * l + ch : 3 * l + ch + 1, :] = over_cameras(basis[l] * dcol[ch])
    xx, yy, zz, xy, yz, xz = x * x, y * y, z * z, x * y, y * z, x * z
    dx = (
        -C1 * e[3]
        + C20 * y * e[4]
        + x * (2.0 * C24 * e[8] - 2.0 * C22 * e[6])
        + C23 * z * e[7]
        + xy * (6.0 * C30 * e[9] - 2.0 * C32 * e[11])
        + C31 * yz * e[10]
        + xz * (2.0 * C35 * e[14] - 6.0 * C33 * e[12])
        + C34 * (4.0 * zz - 3.0 * xx - yy) * e[13]
        + 3.0 * C36 * (xx - yy) * e[15]
    )
    dy = (
        -C1 * e[1]
        + C20 * x * e[4]
        + C21 * z * e[5]
        - y * (2.0 * C22 * e[6] + 2.0 * C24 * e[8])
        + 3.0 * C30 * (xx - yy) * e[9]
        + C31 * xz * e[10]
        + C32 * (4.0 * zz - xx - 3.0 * yy) * e[11]
        - yz * (6.0 * C33 * e[12] + 2.0 * C35 * e[14])
        - xy * (2.0 * C34 * e[13] + 6.0 * C36 * e[15])
    )
    dz = (
        C1 * e[2]
        + C21 * y * e[5]
        + 4.0 * C22 * z * e[6]
        + C23 * x * e[7]
        + C31 * xy * e[10]
        + 8.0 * C32 * yz * e[11]
        + C33 * (6.0 * zz - 3.0 * xx - 3.0 * yy) * e[12]
        + 8.0 * C34 * xz * e[13]
        + C35 * (xx - yy) * e[14]
    )
    along = x * dx + y * dy + z * dz
    doff = [inv_len * (dx - x * along), inv_len * (dy - y * along), inv_len * (dz - z * along)]
    ca, cb, cc = conic
    s = dca * ca + dcb * cb + dcc * cc
    da = inv_det * dcc - s * ca
    dc = inv_det * dca - s * cc
    db = -(inv_det * dcb) - 2.0 * s * cb
    da2, dc2 = da + da, dc + dc
    ds0 = [da2 * s0[k] + db * s1[k] for k in range(3)]
    ds1 = [dc2 * s1[k] + db * s0[k] for k in range(3)]
    dt0 = [sum(ds0[k] * factor[c][k] for k in range(3)) for c in range(3)]
    dt1 = [sum(ds1[k] * factor[c][k] for k in range(3)) for c in range(3)]
    dfactor = [[over_cameras(t0[c] * ds0[k] + t1[c] * ds1[k]) for k in range(3)] for c in range(3)]
    n0 = sum(dt0[c] * rot[2][c] for c in range(3))
    n1 = sum(dt1[c] * rot[2][c] for c in range(3))
    m0 = sum(dt0[c] * rot[0][c] for c in range(3))
    m1 = sum(dt1[c] * rot[1][c] for c in range(3))
    dfiz = (m0 - tx * n0) + (m1 - ty * n1)
    dtx = focal * du - fiz * n0
    dty = focal * dv - fiz * n1
    dp = [dtx * iz, dty * iz, -iz * (fiz * dfiz + dtx * tx + dty * ty)]
    dcenters = [
        over_cameras(sum(rot[r][c] * dp[r] for r in range(3)) + doff[c]) for c in range(3)
    ]
    return dcenters, dfactor


def shape_back(unit, inv, stretch, factor, dfactor):
    w, x, y, z = unit
    dscale = [sum(factor[r][k] * dfactor[r][k] for r in range(3)) for k in range(3)]
    d = [[dfactor[r][k] * stretch[k] for k in range(3)] for r in range(3)]
    dw = 2.0 * (z * (d[1][0] - d[0][1]) + y * (d[0][2] - d[2][0]) + x * (d[2][1] - d[1][2]))
    dx = 2.0 * (
        y * (d[0][1] + d[1][0]) + z * (d[0][2] + d[2][0]) + w * (d[2][1] - d[1][2])
    ) - 4.0 * x * (d[1][1] + d[2][2])
    dy = 2.0 * (
        x * (d[0][1] + d[1][0]) + z * (d[1][2] + d[2][1]) + w * (d[0][2] - d[2][0])
    ) - 4.0 * y * (d[0][0] + d[2][2])
    dz = 2.0 * (
        x * (d[0][2] + d[2][0]) + y * (d[1][2] + d[2][1]) + w * (d[1][0] - d[0][1])
    ) - 4.0 * z * (d[0][0] + d[1][1])
    along = w * dw + x * dx + y * dy + z * dz
    dquat = [inv * (g - q * along) for g, q in zip((dw, dx, dy, dz), unit)]
    return dscale, dquat


def lane_pick(table, lanes):
    return jnp.take_along_axis(table, lanes, axis=1, mode="promise_in_bounds")


def triangle(later):
    row = lax.broadcasted_iota(jnp.int32, (PIX, PIX), 0)
    col = lax.broadcasted_iota(jnp.int32, (PIX, PIX), 1)
    return jnp.where(row > col if later else row < col, 1.0, 0.0).astype(BF16)


def render_tile(geometry, opacity, count, tile, grad, grad_t, before, after):
    entry = lax.broadcasted_iota(jnp.int32, (1, PIX), 1)
    live = jnp.where(entry < count, opacity, 0.0)
    left = (16 * lax.rem(tile, TW) + 8).astype(F32)
    top = (16 * lax.div(tile, TW) + 8).astype(F32)
    u, v = geometry[0:1] - left, geometry[1:2] - top
    ca, cb, cc = geometry[2:3], geometry[3:4], geometry[4:5]
    colour = geometry[5:8]
    local = lax.broadcasted_iota(jnp.int32, (16, PIX), 0).astype(F32) - 7.5
    dx, dy = local - u, local - v
    part_a = (-0.5 * LOG2E * ca) * dx * dx
    part_b = (-LOG2E * cb) * dx
    part_c = (-0.5 * LOG2E * cc) * dy * dy
    c_hi, c_lo = split_two(colour)
    mix = jnp.concatenate([c_hi, c_lo, c_hi], axis=0)
    reach = dot(grad_t, mix)
    moments = [None, None, None]
    w_hi_all, w_lo_all = [], []
    for at in range(0, 16, 4):
        alphas, logs = [], []
        for line in range(at, at + 4):
            power = part_a + part_b * dy[line : line + 1] + part_c[line : line + 1]
            alphas.append(live * jnp.exp2(power))
        alpha = jnp.concatenate(alphas, axis=0)
        left_over = 1.0 - alpha
        log_left = jnp.log2(left_over)
        log_hi, log_lo = split_two(log_left)
        weight = alpha * jnp.exp2(dot(log_hi, before) + dot(log_lo, before))
        gain = weight * reach[16 * at : 16 * at + 64]
        g_hi, g_lo = split_two(gain)
        behind = dot(g_hi, after) + dot(g_lo, after)
        back = gain - behind * (alpha / left_over)
        w_hi, w_lo = split_two(weight)
        w_hi_all.append(w_hi)
        w_lo_all.append(w_lo)
        for k in range(4):
            piece = back[16 * k : 16 * k + 16]
            level = at + k - 7.5
            terms = (piece, level * piece, (level * level) * piece)
            for m in range(3):
                moments[m] = terms[m] if moments[m] is None else moments[m] + terms[m]
    w_hi = jnp.concatenate(w_hi_all, axis=0)
    w_lo = jnp.concatenate(w_lo_all, axis=0)
    both = jnp.concatenate([c_hi, c_lo], axis=0)
    first = dot_nt(both, w_hi)
    picture = first[0:3] + first[3:6] + dot_nt(c_hi, w_lo)
    pg_hi, pg_lo = split_two(grad)
    both = jnp.concatenate([pg_hi, pg_lo], axis=0)
    first = dot(both, w_hi)
    dcolour = first[0:3] + first[3:6] + dot(pg_hi, w_lo)

    def total(value):
        return jnp.sum(value, axis=0, keepdims=True)

    m0, my, myy = (total(m) for m in moments)
    mx, mxy = total(local * moments[0]), total(local * moments[1])
    mxx = total(local * local * moments[0])
    qx, qy = mx - u * m0, my - v * m0
    qxx = mxx - u * (mx + qx)
    qyy = myy - v * (my + qy)
    qxy = mxy - u * my - v * qx
    grads = [
        ca * qx + cb * qy,
        cb * qx + cc * qy,
        -0.5 * qxx,
        -qxy,
        -0.5 * qyy,
        dcolour[0:1],
        dcolour[1:2],
        dcolour[2:3],
        m0 / opacity,
    ]
    return picture, grads


def exchange(axis, me, size, source, landing, send_sem, recv_sem):
    def copy(peer, slot):
        return pltpu.make_async_remote_copy(
            src_ref=source(peer),
            dst_ref=landing.at[slot],
            send_sem=send_sem.at[peer],
            recv_sem=recv_sem.at[slot],
            device_id={axis: peer},
            device_id_type=pl.DeviceIdType.MESH,
        )

    def start(step, carry):
        copy(lax.rem(me + step, size), me).start()
        return carry

    def sent(step, carry):
        copy(lax.rem(me + step, size), me).wait_send()
        return carry

    lax.fori_loop(1, size, start, 0)

    def arrived(peer):
        copy(peer, peer).wait_recv()

    return arrived, lambda: lax.fori_loop(1, size, sent, 0)


def greet(axis, me, size, barrier):
    def signal(step, carry):
        pl.semaphore_signal(
            barrier,
            inc=1,
            device_id={axis: lax.rem(me + step, size)},
            device_id_type=pl.DeviceIdType.MESH,
        )
        return carry

    lax.fori_loop(1, size, signal, 0)


def picker(index, size):
    blocks = index.shape[0]
    high, low = lax.shift_right_logical(index, 7), lax.bitwise_and(index, 127)
    highs = [jnp.broadcast_to(high[b : b + 1], (8, LANES)) for b in range(blocks)]
    lows = [jnp.broadcast_to(low[b : b + 1], (8, LANES)) for b in range(blocks)]

    def add(number, table, picks):
        geometry, opacity = picks
        front = table[0:8]
        last = jnp.broadcast_to(table[8:9], (8, LANES))
        geometry = tuple(
            jnp.where(highs[b] == number, lane_pick(front, lows[b]), geometry[b])
            for b in range(blocks)
        )
        opacity = tuple(
            jnp.where(
                high[8 * g : 8 * g + 8] == number, lane_pick(last, low[8 * g : 8 * g + 8]), opacity[g]
            )
            for g in range(blocks // 8)
        )
        return geometry, opacity

    zero = jnp.zeros((8, LANES), F32)
    return add, ((zero,) * blocks, (zero,) * (blocks // 8))


def scatter_sides(index, groups):
    count = index.shape[1]
    high, low = lax.shift_right_logical(index, 8), lax.bitwise_and(index, 255)
    mask = lax.broadcasted_iota(jnp.int32, (groups, count), 0) == high
    hot = lax.broadcasted_iota(jnp.int32, (256, count), 0) == low
    return mask, jnp.where(hot, 1.0, 0.0).astype(BF16)


def scatter(rows, mask, hot):
    groups = mask.shape[0]
    sides, owners = [], []
    for r, row in enumerate(rows):
        for _ in range(3 if r in FINE_ROWS else 2):
            high = row.astype(BF16).astype(F32)
            sides.append(jnp.where(mask, high, 0.0))
            owners.append(r)
            row = row - high
    if len(sides) * groups % 16:
        sides.append(jnp.zeros_like(sides[0]))
    out = dot_nt(jnp.concatenate(sides, axis=0).astype(BF16), hot)
    return [
        sum(out[groups * k : groups * (k + 1)] for k, owner in enumerate(owners) if owner == r)
        for r in range(len(rows))
    ]


def train_kernel(
    n_img,
    n_view,
    sizes,
    cameras_ref,
    centers_ref,
    scales_ref,
    quats_ref,
    logits_ref,
    harm_ref,
    lists_ref,
    counts_ref,
    ids_ref,
    slots_ref,
    grad_ref,
    picture_ref,
    out_centers_ref,
    out_scales_ref,
    out_quats_ref,
    out_logits_ref,
    out_harm_ref,
    send_one,
    recv_one,
    send_two,
    recv_two,
    send_three,
    recv_three,
    send_four,
    recv_four,
    view_sems,
    img_sems,
):
    focal, half_w, half_h = sizes
    img, view = lax.axis_index("img"), lax.axis_index("view")
    barrier = pltpu.get_barrier_semaphore()
    greet("view", view, n_view, barrier)
    greet("img", img, n_img, barrier)

    rot = rotations(cameras_ref[...], n_view)
    centers = [centers_ref[c : c + 1, :] for c in range(3)]
    unit, inv_norm, stretch, factor = shape_factor(
        [quats_ref[k : k + 1, :] for k in range(4)], [scales_ref[k : k + 1, :] for k in range(3)]
    )
    opacity = 1.0 / (1.0 + jnp.exp(-logits_ref[...]))
    values, saved = project(rot, centers, factor, harm_ref, focal, half_w, half_h)
    for r, value in enumerate(values):
        send_one[:, r, :] = value
    send_one[:, 8, :] = jnp.broadcast_to(opacity, (n_view, LANES))

    pl.semaphore_wait(barrier, n_view + n_img - 2)
    arrived, sent_one = exchange(
        "view", view, n_view, lambda p: send_one.at[p], recv_one, view_sems.at[0], view_sems.at[1]
    )

    add, picks = picker(slots_ref[...], n_view)
    picks = add(view, send_one[view], picks)

    def take_view(step, picks):
        peer = lax.rem(view + step, n_view)
        arrived(peer)
        return add(peer, recv_one[peer], picks)

    geometry, last = lax.fori_loop(1, n_view, take_view, picks)
    for d in range(n_img):
        send_two[d, 0:8, :] = geometry[d]
        send_two[d, 8:9, :] = last[d // 8][d % 8 : d % 8 + 1]

    arrived, sent_two = exchange(
        "img", img, n_img, lambda p: send_two.at[p], recv_two, img_sems.at[0], img_sems.at[1]
    )

    tiles = lists_ref.shape[0]
    lists = lists_ref[...]
    blocks = jnp.concatenate(
        [lists[t : t + 1, LANES * h : LANES * h + LANES] for t in range(tiles) for h in range(2)], axis=0
    )
    entry_index = jnp.concatenate([lists[t : t + 1] for t in range(tiles)], axis=1)
    entry_mask, entry_hot = scatter_sides(entry_index, n_img // 2)
    before, after = triangle(False), triangle(True)
    add, picks = picker(blocks, n_img)
    picks = add(img, send_two[img], picks)

    def take_img(step, picks):
        peer = lax.rem(img + step, n_img)
        arrived(peer)
        return add(peer, recv_two[peer], picks)

    geometry, last = lax.fori_loop(1, n_img, take_img, picks)
    row_grads = [[] for _ in range(ROWS)]
    for t in range(tiles):
        entries = jnp.concatenate([geometry[2 * t], geometry[2 * t + 1]], axis=1)
        solid = jnp.concatenate([last[0][2 * t : 2 * t + 1], last[0][2 * t + 1 : 2 * t + 2]], axis=1)
        grad = grad_ref[t]
        high = grad.astype(BF16).astype(F32)
        grad_t = jnp.concatenate([high, high, grad - high], axis=0).T.astype(BF16)
        picture, grads = render_tile(
            entries, solid, counts_ref[t], ids_ref[t], grad, grad_t, before, after
        )
        picture_ref[t] = picture
        for r in range(ROWS):
            row_grads[r].append(grads[r])

    rows = [jnp.concatenate(parts, axis=1) for parts in row_grads]
    for r, total in enumerate(scatter(rows, entry_mask, entry_hot)):
        for h in range(2):
            send_three[:, h, r, :] = total[:, LANES * h : LANES * h + LANES]
    arrived, sent_three = exchange(
        "img",
        img,
        n_img,
        lambda p: send_three.at[lax.div(p, 2), lax.rem(p, 2)],
        recv_three,
        img_sems.at[2],
        img_sems.at[3],
    )
    recv_three[img] = send_three[lax.div(img, 2), lax.rem(img, 2)]
    slot_index = jnp.concatenate([slots_ref[d : d + 1, :] for d in range(n_img)], axis=1)
    slot_mask, slot_hot = scatter_sides(slot_index, n_view // 2)

    def take_back(step, carry):
        arrived(lax.rem(img + step, n_img))
        return carry

    lax.fori_loop(1, n_img, take_back, 0)

    rows = [
        jnp.concatenate([recv_three[d, r : r + 1, :] for d in range(n_img)], axis=1) for r in range(ROWS)
    ]
    for r, total in enumerate(scatter(rows, slot_mask, slot_hot)):
        for h in range(2):
            send_four[:, h, r, :] = total[:, LANES * h : LANES * h + LANES]
    arrived, sent_four = exchange(
        "view",
        view,
        n_view,
        lambda p: send_four.at[lax.div(p, 2), lax.rem(p, 2)],
        recv_four,
        view_sems.at[2],
        view_sems.at[3],
    )
    recv_four[view] = send_four[lax.div(view, 2), lax.rem(view, 2)]

    def take_home(step, carry):
        arrived(lax.rem(view + step, n_view))
        return carry

    lax.fori_loop(1, n_view, take_home, 0)

    grads = [recv_four[:, r, :] for r in range(ROWS)]
    dcenters, dfactor = project_back(rot, factor, harm_ref, focal, saved, grads, out_harm_ref)
    dscale, dquat = shape_back(unit, inv_norm, stretch, factor, dfactor)
    for c in range(3):
        out_centers_ref[c : c + 1, :] = dcenters[c]
        out_scales_ref[c : c + 1, :] = dscale[c]
    for k in range(4):
        out_quats_ref[k : k + 1, :] = dquat[k]
    out_logits_ref[...] = over_cameras(grads[8]) * opacity * (1.0 - opacity)
    sent_one()
    sent_two()
    sent_three()
    sent_four()


def per_device(
    centers,
    log_scales,
    quaternions,
    logits,
    harmonics,
    cameras,
    tile_lists,
    tile_counts,
    tile_ids,
    send_index,
    pixel_grad,
):
    n_img, n_view = lax.axis_size("img"), lax.axis_size("view")
    tiles = tile_ids.shape[2]
    sizes = (16.0 * TW, 8.0 * TW, 8.0 * (n_img * tiles // TW))
    vmem, smem = pl.BlockSpec(memory_space=pltpu.VMEM), pl.BlockSpec(memory_space=pltpu.SMEM)
    per_view, per_img = (n_view, ROWS, LANES), (n_img, ROWS, LANES)
    out = pl.pallas_call(
        functools.partial(train_kernel, n_img, n_view, sizes),
        out_shape=(
            jax.ShapeDtypeStruct((tiles, 3, PIX), F32),
            jax.ShapeDtypeStruct((3, LANES), F32),
            jax.ShapeDtypeStruct((3, LANES), F32),
            jax.ShapeDtypeStruct((4, LANES), F32),
            jax.ShapeDtypeStruct((1, LANES), F32),
            jax.ShapeDtypeStruct((48, LANES), F32),
        ),
        in_specs=[vmem] * 7 + [smem] * 2 + [vmem] * 2,
        out_specs=(vmem,) * 6,
        scratch_shapes=[
            pltpu.VMEM(per_view, F32),
            pltpu.VMEM(per_view, F32),
            pltpu.VMEM(per_img, F32),
            pltpu.VMEM(per_img, F32),
            pltpu.VMEM((n_img // 2, 2, ROWS, LANES), F32),
            pltpu.VMEM(per_img, F32),
            pltpu.VMEM((n_view // 2, 2, ROWS, LANES), F32),
            pltpu.VMEM(per_view, F32),
            pltpu.SemaphoreType.DMA((4, n_view)),
            pltpu.SemaphoreType.DMA((4, n_img)),
        ],
        compiler_params=pltpu.CompilerParams(
            collective_id=0, has_side_effects=True, vmem_limit_bytes=40 * 1024 * 1024
        ),
    )(
        cameras,
        centers,
        log_scales,
        quaternions,
        logits.reshape(1, -1),
        harmonics,
        tile_lists[0, 0],
        tile_counts[0, 0],
        tile_ids[0, 0],
        send_index[0, 0],
        pixel_grad[0, 0],
    )
    return (out[0][None, None], out[1], out[2], out[3], out[4].reshape(-1), out[5])


def solution(mesh):
    split = P(None, ("img", "view"))
    placed = (
        split,
        split,
        split,
        P(("img", "view")),
        split,
        P(),
        P("view", "img", None, None),
        P("view", "img", None),
        P("view", "img", None),
        P("view", "img", None, None),
        P("view", "img", None, None, None),
    )
    return jax.shard_map(
        per_device,
        mesh=mesh,
        in_specs=placed,
        out_specs=(P("view", "img", None, None, None), split, split, split, P(("img", "view")), split),
        check_vma=False,
    )
```

```python
import functools

import jax
import jax.numpy as jnp
from jax import lax
from jax.experimental import pallas as pl
from jax.experimental.pallas import tpu as pltpu
from jax.sharding import PartitionSpec as P

TW = 8
ROWS = 9
LANES = 128
PIX = 256
MINOR = {"view": 4, "img": 2}
FINE_ROWS = (2, 3, 4)
LOG2E = 1.4426950408889634
CAMERA_DISTANCE = 4.0
C0 = 0.28209479177387814
C1 = 0.4886025119029199
C20, C21, C22, C23, C24 = (
    1.0925484305920792,
    -1.0925484305920792,
    0.31539156525252005,
    -1.0925484305920792,
    0.5462742152960396,
)
C30, C31, C32, C33, C34, C35, C36 = (
    -0.5900435899266435,
    2.890611442640554,
    -0.4570457994644658,
    0.3731763325901154,
    -0.4570457994644658,
    1.445305721320277,
    -0.5900435899266435,
)
F32 = jnp.float32
BF16 = jnp.bfloat16


def split_two(value):
    high = value.astype(BF16)
    low = (value - high.astype(F32)).astype(BF16)
    return high, low


def dot(left, right):
    return lax.dot_general(left, right, (((1,), (0,)), ((), ())), preferred_element_type=F32)


def dot_nt(left, right):
    return lax.dot_general(left, right, (((1,), (1,)), ((), ())), preferred_element_type=F32)


def rotations(cameras, count):
    turns = jnp.concatenate([jnp.cos(cameras), jnp.sin(cameras)], axis=0).T
    ca, cb, cg, sa, sb, sg = (
        jnp.broadcast_to(turns[:, k : k + 1], (count, LANES)) for k in range(6)
    )
    return [
        [cg * ca, cg * sa * sb - sg * cb, cg * sa * cb + sg * sb],
        [sg * ca, sg * sa * sb + cg * cb, sg * sa * cb - cg * sb],
        [-sa, ca * sb, ca * cb],
    ]


def shape_factor(quats, scales):
    inv = lax.rsqrt(sum(q * q for q in quats))
    w, x, y, z = (q * inv for q in quats)
    rot = [
        [1.0 - 2.0 * (y * y + z * z), 2.0 * (x * y - w * z), 2.0 * (x * z + w * y)],
        [2.0 * (x * y + w * z), 1.0 - 2.0 * (x * x + z * z), 2.0 * (y * z - w * x)],
        [2.0 * (x * z - w * y), 2.0 * (y * z + w * x), 1.0 - 2.0 * (x * x + y * y)],
    ]
    stretch = [jnp.exp(s) for s in scales]
    factor = [[rot[r][k] * stretch[k] for k in range(3)] for r in range(3)]
    return (w, x, y, z), inv, stretch, factor


def basis_of(x, y, z):
    xx, yy, zz = x * x, y * y, z * z
    return [
        None,
        -C1 * y,
        C1 * z,
        -C1 * x,
        C20 * x * y,
        C21 * y * z,
        C22 * (2.0 * zz - xx - yy),
        C23 * x * z,
        C24 * (xx - yy),
        C30 * y * (3.0 * xx - yy),
        C31 * x * y * z,
        C32 * y * (4.0 * zz - xx - yy),
        C33 * z * (2.0 * zz - 3.0 * xx - 3.0 * yy),
        C34 * x * (4.0 * zz - xx - yy),
        C35 * z * (xx - yy),
        C36 * x * (xx - 3.0 * yy),
    ]


def project(rot, centers, factor, harm_ref, focal, half_w, half_h):
    pts = [rot[r][0] * centers[0] + rot[r][1] * centers[1] + rot[r][2] * centers[2] for r in range(3)]
    iz = 1.0 / (pts[2] + CAMERA_DISTANCE)
    fiz = focal * iz
    tx, ty = pts[0] * iz, pts[1] * iz
    t0 = [fiz * (rot[0][c] - tx * rot[2][c]) for c in range(3)]
    t1 = [fiz * (rot[1][c] - ty * rot[2][c]) for c in range(3)]
    s0 = [t0[0] * factor[0][k] + t0[1] * factor[1][k] + t0[2] * factor[2][k] for k in range(3)]
    s1 = [t1[0] * factor[0][k] + t1[1] * factor[1][k] + t1[2] * factor[2][k] for k in range(3)]
    cov_a = s0[0] * s0[0] + s0[1] * s0[1] + s0[2] * s0[2] + 0.3
    cov_b = s0[0] * s1[0] + s0[1] * s1[1] + s0[2] * s1[2]
    cov_c = s1[0] * s1[0] + s1[1] * s1[1] + s1[2] * s1[2] + 0.3
    inv_det = 1.0 / (cov_a * cov_c - cov_b * cov_b)
    conic = (cov_c * inv_det, -cov_b * inv_det, cov_a * inv_det)
    offs = [centers[c] + CAMERA_DISTANCE * rot[2][c] for c in range(3)]
    inv_len = lax.rsqrt(offs[0] * offs[0] + offs[1] * offs[1] + offs[2] * offs[2])
    x, y, z = (o * inv_len for o in offs)
    basis = basis_of(x, y, z)
    shade = []
    for ch in range(3):
        total = 0.5 + C0 * harm_ref[ch : ch + 1, :]
        for l in range(1, 16):
            total = total + basis[l] * harm_ref[3 * l + ch : 3 * l + ch + 1, :]
        shade.append(total)
    colour = [jnp.maximum(s, 0.0) for s in shade]
    values = [focal * tx + half_w, focal * ty + half_h, *conic, *colour]
    saved = (iz, fiz, tx, ty, t0, t1, s0, s1, conic, inv_det, inv_len, (x, y, z), basis, shade)
    return values, saved


def over_cameras(value):
    return jnp.sum(value, axis=0, keepdims=True)


def project_back(rot, factor, harm_ref, focal, saved, grads, grad_harm_ref):
    iz, fiz, tx, ty, t0, t1, s0, s1, conic, inv_det, inv_len, (x, y, z), basis, shade = saved
    du, dv, dca, dcb, dcc = grads[:5]
    dcol = []
    for ch in range(3):
        g = grads[5 + ch]
        dcol.append(jnp.where(shade[ch] > 0.0, g, jnp.where(shade[ch] == 0.0, 0.5 * g, 0.0)))
    e = [None]
    for ch in range(3):
        grad_harm_ref[ch : ch + 1, :] = C0 * over_cameras(dcol[ch])
    for l in range(1, 16):
        e.append(sum(harm_ref[3 * l + ch : 3 * l + ch + 1, :] * dcol[ch] for ch in range(3)))
        for ch in range(3):
            grad_harm_ref[3 * l + ch : 3 * l + ch + 1, :] = over_cameras(basis[l] * dcol[ch])
    xx, yy, zz, xy, yz, xz = x * x, y * y, z * z, x * y, y * z, x * z
    dx = (
        -C1 * e[3]
        + C20 * y * e[4]
        + x * (2.0 * C24 * e[8] - 2.0 * C22 * e[6])
        + C23 * z * e[7]
        + xy * (6.0 * C30 * e[9] - 2.0 * C32 * e[11])
        + C31 * yz * e[10]
        + xz * (2.0 * C35 * e[14] - 6.0 * C33 * e[12])
        + C34 * (4.0 * zz - 3.0 * xx - yy) * e[13]
        + 3.0 * C36 * (xx - yy) * e[15]
    )
    dy = (
        -C1 * e[1]
        + C20 * x * e[4]
        + C21 * z * e[5]
        - y * (2.0 * C22 * e[6] + 2.0 * C24 * e[8])
        + 3.0 * C30 * (xx - yy) * e[9]
        + C31 * xz * e[10]
        + C32 * (4.0 * zz - xx - 3.0 * yy) * e[11]
        - yz * (6.0 * C33 * e[12] + 2.0 * C35 * e[14])
        - xy * (2.0 * C34 * e[13] + 6.0 * C36 * e[15])
    )
    dz = (
        C1 * e[2]
        + C21 * y * e[5]
        + 4.0 * C22 * z * e[6]
        + C23 * x * e[7]
        + C31 * xy * e[10]
        + 8.0 * C32 * yz * e[11]
        + C33 * (6.0 * zz - 3.0 * xx - 3.0 * yy) * e[12]
        + 8.0 * C34 * xz * e[13]
        + C35 * (xx - yy) * e[14]
    )
    along = x * dx + y * dy + z * dz
    doff = [inv_len * (dx - x * along), inv_len * (dy - y * along), inv_len * (dz - z * along)]
    ca, cb, cc = conic
    s = dca * ca + dcb * cb + dcc * cc
    da = inv_det * dcc - s * ca
    dc = inv_det * dca - s * cc
    db = -(inv_det * dcb) - 2.0 * s * cb
    da2, dc2 = da + da, dc + dc
    ds0 = [da2 * s0[k] + db * s1[k] for k in range(3)]
    ds1 = [dc2 * s1[k] + db * s0[k] for k in range(3)]
    dt0 = [sum(ds0[k] * factor[c][k] for k in range(3)) for c in range(3)]
    dt1 = [sum(ds1[k] * factor[c][k] for k in range(3)) for c in range(3)]
    dfactor = [[over_cameras(t0[c] * ds0[k] + t1[c] * ds1[k]) for k in range(3)] for c in range(3)]
    n0 = sum(dt0[c] * rot[2][c] for c in range(3))
    n1 = sum(dt1[c] * rot[2][c] for c in range(3))
    m0 = sum(dt0[c] * rot[0][c] for c in range(3))
    m1 = sum(dt1[c] * rot[1][c] for c in range(3))
    dfiz = (m0 - tx * n0) + (m1 - ty * n1)
    dtx = focal * du - fiz * n0
    dty = focal * dv - fiz * n1
    dp = [dtx * iz, dty * iz, -iz * (fiz * dfiz + dtx * tx + dty * ty)]
    dcenters = [
        over_cameras(sum(rot[r][c] * dp[r] for r in range(3)) + doff[c]) for c in range(3)
    ]
    return dcenters, dfactor


def shape_back(unit, inv, stretch, factor, dfactor):
    w, x, y, z = unit
    dscale = [sum(factor[r][k] * dfactor[r][k] for r in range(3)) for k in range(3)]
    d = [[dfactor[r][k] * stretch[k] for k in range(3)] for r in range(3)]
    dw = 2.0 * (z * (d[1][0] - d[0][1]) + y * (d[0][2] - d[2][0]) + x * (d[2][1] - d[1][2]))
    dx = 2.0 * (
        y * (d[0][1] + d[1][0]) + z * (d[0][2] + d[2][0]) + w * (d[2][1] - d[1][2])
    ) - 4.0 * x * (d[1][1] + d[2][2])
    dy = 2.0 * (
        x * (d[0][1] + d[1][0]) + z * (d[1][2] + d[2][1]) + w * (d[0][2] - d[2][0])
    ) - 4.0 * y * (d[0][0] + d[2][2])
    dz = 2.0 * (
        x * (d[0][2] + d[2][0]) + y * (d[1][2] + d[2][1]) + w * (d[1][0] - d[0][1])
    ) - 4.0 * z * (d[0][0] + d[1][1])
    along = w * dw + x * dx + y * dy + z * dz
    dquat = [inv * (g - q * along) for g, q in zip((dw, dx, dy, dz), unit)]
    return dscale, dquat


def lane_pick(table, lanes):
    return jnp.take_along_axis(table, lanes, axis=1, mode="promise_in_bounds")


def triangle(later):
    row = lax.broadcasted_iota(jnp.int32, (PIX, PIX), 0)
    col = lax.broadcasted_iota(jnp.int32, (PIX, PIX), 1)
    return jnp.where(row > col if later else row < col, 1.0, 0.0).astype(BF16)


def render_tile(geometry, opacity, count, tile, grad, grad_t, before, after):
    entry = lax.broadcasted_iota(jnp.int32, (1, PIX), 1)
    live = jnp.where(entry < count, opacity, 0.0)
    left = (16 * lax.rem(tile, TW) + 8).astype(F32)
    top = (16 * lax.div(tile, TW) + 8).astype(F32)
    u, v = geometry[0:1] - left, geometry[1:2] - top
    ca, cb, cc = geometry[2:3], geometry[3:4], geometry[4:5]
    colour = geometry[5:8]
    local = lax.broadcasted_iota(jnp.int32, (16, PIX), 0).astype(F32) - 7.5
    dx, dy = local - u, local - v
    part_a = (-0.5 * LOG2E * ca) * dx * dx
    part_b = (-LOG2E * cb) * dx
    part_c = (-0.5 * LOG2E * cc) * dy * dy
    c_hi, c_lo = split_two(colour)
    mix = jnp.concatenate([c_hi, c_lo, c_hi], axis=0)
    reach = dot(grad_t, mix)
    moments = [None, None, None]
    w_hi_all, w_lo_all = [], []
    for at in range(0, 16, 4):
        alphas, logs = [], []
        for line in range(at, at + 4):
            power = part_a + part_b * dy[line : line + 1] + part_c[line : line + 1]
            alphas.append(live * jnp.exp2(power))
        alpha = jnp.concatenate(alphas, axis=0)
        left_over = 1.0 - alpha
        log_left = jnp.log2(left_over)
        log_hi, log_lo = split_two(log_left)
        weight = alpha * jnp.exp2(dot(log_hi, before) + dot(log_lo, before))
        gain = weight * reach[16 * at : 16 * at + 64]
        g_hi, g_lo = split_two(gain)
        behind = dot(g_hi, after) + dot(g_lo, after)
        back = gain - behind * (alpha / left_over)
        w_hi, w_lo = split_two(weight)
        w_hi_all.append(w_hi)
        w_lo_all.append(w_lo)
        for k in range(4):
            piece = back[16 * k : 16 * k + 16]
            level = at + k - 7.5
            terms = (piece, level * piece, (level * level) * piece)
            for m in range(3):
                moments[m] = terms[m] if moments[m] is None else moments[m] + terms[m]
    w_hi = jnp.concatenate(w_hi_all, axis=0)
    w_lo = jnp.concatenate(w_lo_all, axis=0)
    both = jnp.concatenate([c_hi, c_lo], axis=0)
    first = dot_nt(both, w_hi)
    picture = first[0:3] + first[3:6] + dot_nt(c_hi, w_lo)
    pg_hi, pg_lo = split_two(grad)
    both = jnp.concatenate([pg_hi, pg_lo], axis=0)
    first = dot(both, w_hi)
    dcolour = first[0:3] + first[3:6] + dot(pg_hi, w_lo)

    def total(value):
        return jnp.sum(value, axis=0, keepdims=True)

    m0, my, myy = (total(m) for m in moments)
    mx, mxy = total(local * moments[0]), total(local * moments[1])
    mxx = total(local * local * moments[0])
    qx, qy = mx - u * m0, my - v * m0
    qxx = mxx - u * (mx + qx)
    qyy = myy - v * (my + qy)
    qxy = mxy - u * my - v * qx
    grads = [
        ca * qx + cb * qy,
        cb * qx + cc * qy,
        -0.5 * qxx,
        -qxy,
        -0.5 * qyy,
        dcolour[0:1],
        dcolour[1:2],
        dcolour[2:3],
        m0 / opacity,
    ]
    return picture, grads


def ring(size, steps):
    return min(steps, size - steps)


def farthest_first(axis, size):
    minor = MINOR[axis]
    major = size // minor
    offsets = [(a, b) for a in range(major) for b in range(minor) if a or b]
    return sorted(offsets, key=lambda o: -ring(major, o[0]) - ring(minor, o[1]) * (axis == "view"))


def neighbour(me, offset, axis, size):
    minor = MINOR[axis]
    major = size // minor

    def wrap(value, limit):
        return jnp.where(value >= limit, value - limit, value)

    return wrap(lax.div(me, minor) + offset[0], major) * minor + wrap(
        lax.rem(me, minor) + offset[1], minor
    )


def exchange(axis, me, size, source, landing, send_sem, recv_sem):
    peers = [neighbour(me, offset, axis, size) for offset in farthest_first(axis, size)]

    def copy(peer, slot):
        return pltpu.make_async_remote_copy(
            src_ref=source(peer),
            dst_ref=landing.at[slot],
            send_sem=send_sem.at[peer],
            recv_sem=recv_sem.at[slot],
            device_id={axis: peer},
            device_id_type=pl.DeviceIdType.MESH,
        )

    for peer in peers:
        copy(peer, me).start()

    def arrived(peer):
        copy(peer, peer).wait_recv()

    def sent():
        for peer in peers:
            copy(peer, me).wait_send()

    return peers[::-1], arrived, sent


def greet(axis, me, size, barrier):
    for offset in farthest_first(axis, size):
        pl.semaphore_signal(
            barrier,
            inc=1,
            device_id={axis: neighbour(me, offset, axis, size)},
            device_id_type=pl.DeviceIdType.MESH,
        )


def split_rows(block):
    parts, lasts = [], []
    front, last = block[0:8], block[8:9]
    for _ in range(3):
        parts.append(front.astype(BF16).astype(F32))
        lasts.append(last.astype(BF16).astype(F32))
        front, last = front - parts[-1], last - lasts[-1]
    filler = jnp.zeros((5, LANES), F32)
    return jnp.concatenate(parts + lasts + [filler], axis=0).astype(BF16)


def pick(table_ref, high, hot):
    groups = table_ref.shape[1]
    table = jnp.concatenate(
        [table_ref[half].reshape(32 * groups, LANES) for half in range(2)], axis=1
    )
    found = dot(table, hot)
    total = sum(
        jnp.where(high == g, found[32 * g : 32 * g + 32], 0.0) for g in range(groups)
    )
    return total[0:8] + total[8:16] + total[16:24], total[24:25] + total[25:26] + total[26:27]


def scatter_sides(index, groups):
    count = index.shape[1]
    high, low = lax.shift_right_logical(index, 8), lax.bitwise_and(index, 255)
    mask = lax.broadcasted_iota(jnp.int32, (groups, count), 0) == high
    hot = lax.broadcasted_iota(jnp.int32, (256, count), 0) == low
    return high, mask, jnp.where(hot, 1.0, 0.0).astype(BF16)


def scatter(rows, mask, hot):
    groups = mask.shape[0]
    sides, owners = [], []
    for r, row in enumerate(rows):
        for _ in range(3 if r in FINE_ROWS else 2):
            high = row.astype(BF16).astype(F32)
            sides.append(jnp.where(mask, high, 0.0))
            owners.append(r)
            row = row - high
    if len(sides) * groups % 16:
        sides.append(jnp.zeros_like(sides[0]))
    out = dot_nt(jnp.concatenate(sides, axis=0).astype(BF16), hot)
    return [
        sum(out[groups * k : groups * (k + 1)] for k, owner in enumerate(owners) if owner == r)
        for r in range(len(rows))
    ]


def train_kernel(
    n_img,
    n_view,
    sizes,
    cameras_in,
    centers_in,
    scales_in,
    quats_in,
    logits_in,
    harm_in,
    slots_in,
    lists_in,
    counts_in,
    ids_in,
    grad_in,
    picture_ref,
    out_centers_ref,
    out_scales_ref,
    out_quats_ref,
    out_logits_ref,
    out_harm_ref,
    send_one,
    recv_one,
    send_two,
    recv_two,
    send_three,
    recv_three,
    send_four,
    recv_four,
    cameras_ref,
    centers_ref,
    scales_ref,
    quats_ref,
    logits_ref,
    harm_ref,
    slots_ref,
    lists_ref,
    counts_ref,
    ids_ref,
    grad_ref,
    view_table,
    img_table,
    slot_hot,
    entry_hot,
    view_sems,
    img_sems,
    load_sems,
):
    focal, half_w, half_h = sizes
    img, view = lax.axis_index("img"), lax.axis_index("view")
    barrier = pltpu.get_barrier_semaphore()
    loads = [
        pltpu.make_async_copy(source, target, load_sems.at[k])
        for k, (source, target) in enumerate(
            (
                (cameras_in, cameras_ref),
                (centers_in, centers_ref),
                (scales_in, scales_ref),
                (quats_in, quats_ref),
                (logits_in, logits_ref),
                (harm_in, harm_ref),
                (slots_in, slots_ref),
                (lists_in, lists_ref),
                (counts_in, counts_ref),
                (ids_in, ids_ref),
                (grad_in, grad_ref),
            )
        )
    ]
    for load in loads[:6]:
        load.start()
    greet("view", view, n_view, barrier)
    greet("img", img, n_img, barrier)
    for load in loads[6:]:
        load.start()
    for load in loads[:6]:
        load.wait()

    rot = rotations(cameras_ref[...], n_view)
    centers = [centers_ref[c : c + 1, :] for c in range(3)]
    unit, inv_norm, stretch, factor = shape_factor(
        [quats_ref[k : k + 1, :] for k in range(4)], [scales_ref[k : k + 1, :] for k in range(3)]
    )
    opacity = 1.0 / (1.0 + jnp.exp(-logits_ref[...]))
    values, saved = project(rot, centers, factor, harm_ref, focal, half_w, half_h)
    for r, value in enumerate(values):
        send_one[:, r, :] = value
    send_one[:, 8, :] = jnp.broadcast_to(opacity, (n_view, LANES))

    for load in loads[6:]:
        load.wait()
    pl.semaphore_wait(barrier, n_view + n_img - 2)
    peers, arrived, sent_one = exchange(
        "view", view, n_view, lambda p: send_one.at[p], recv_one, view_sems.at[0], view_sems.at[1]
    )

    slot_index = jnp.concatenate([slots_ref[d : d + 1, :] for d in range(n_img)], axis=1)
    slot_high, slot_mask, hot = scatter_sides(slot_index, n_view // 2)
    slot_hot[...] = hot
    view_table[lax.rem(view, 2), lax.div(view, 2)] = split_rows(send_one[view])
    for at in range(0, n_view - 1, 8):
        for peer in peers[at : at + 8]:
            arrived(peer)
        for peer in peers[at : at + 8]:
            view_table[lax.rem(peer, 2), lax.div(peer, 2)] = split_rows(recv_one[peer])
    geometry, last = pick(view_table, slot_high, slot_hot[...])
    for d in range(n_img):
        send_two[d, 0:8, :] = geometry[:, LANES * d : LANES * d + LANES]
        send_two[d, 8:9, :] = last[:, LANES * d : LANES * d + LANES]

    peers, arrived, sent_two = exchange(
        "img", img, n_img, lambda p: send_two.at[p], recv_two, img_sems.at[0], img_sems.at[1]
    )

    tiles = lists_ref.shape[0]
    lists = lists_ref[...]
    entry_index = jnp.concatenate([lists[t : t + 1] for t in range(tiles)], axis=1)
    entry_high, entry_mask, hot = scatter_sides(entry_index, n_img // 2)
    entry_hot[...] = hot
    before, after = triangle(False), triangle(True)
    img_table[lax.rem(img, 2), lax.div(img, 2)] = split_rows(send_two[img])
    for at in range(0, n_img - 1, 8):
        for peer in peers[at : at + 8]:
            arrived(peer)
        for peer in peers[at : at + 8]:
            img_table[lax.rem(peer, 2), lax.div(peer, 2)] = split_rows(recv_two[peer])
    geometry, last = pick(img_table, entry_high, entry_hot[...])
    row_grads = [[] for _ in range(ROWS)]
    for t in range(tiles):
        entries = geometry[:, PIX * t : PIX * t + PIX]
        solid = last[:, PIX * t : PIX * t + PIX]
        grad = grad_ref[:, t, :]
        high = grad.astype(BF16).astype(F32)
        grad_t = jnp.concatenate([high, high, grad - high], axis=0).T.astype(BF16)
        picture, grads = render_tile(
            entries, solid, counts_ref[t], ids_ref[t], grad, grad_t, before, after
        )
        picture_ref[:, t, :] = picture
        for r in range(ROWS):
            row_grads[r].append(grads[r])

    rows = [jnp.concatenate(parts, axis=1) for parts in row_grads]
    for r, total in enumerate(scatter(rows, entry_mask, entry_hot[...])):
        for h in range(2):
            send_three[:, h, r, :] = total[:, LANES * h : LANES * h + LANES]
    peers, arrived, sent_three = exchange(
        "img",
        img,
        n_img,
        lambda p: send_three.at[lax.div(p, 2), lax.rem(p, 2)],
        recv_three,
        img_sems.at[2],
        img_sems.at[3],
    )
    recv_three[img] = send_three[lax.div(img, 2), lax.rem(img, 2)]
    for peer in peers:
        arrived(peer)

    rows = [
        jnp.concatenate([recv_three[d, r : r + 1, :] for d in range(n_img)], axis=1) for r in range(ROWS)
    ]
    for r, total in enumerate(scatter(rows, slot_mask, slot_hot[...])):
        for h in range(2):
            send_four[:, h, r, :] = total[:, LANES * h : LANES * h + LANES]
    peers, arrived, sent_four = exchange(
        "view",
        view,
        n_view,
        lambda p: send_four.at[lax.div(p, 2), lax.rem(p, 2)],
        recv_four,
        view_sems.at[2],
        view_sems.at[3],
    )
    recv_four[view] = send_four[lax.div(view, 2), lax.rem(view, 2)]

    for peer in peers:
        arrived(peer)

    grads = [recv_four[:, r, :] for r in range(ROWS)]
    dcenters, dfactor = project_back(rot, factor, harm_ref, focal, saved, grads, out_harm_ref)
    dscale, dquat = shape_back(unit, inv_norm, stretch, factor, dfactor)
    for c in range(3):
        out_centers_ref[c : c + 1, :] = dcenters[c]
        out_scales_ref[c : c + 1, :] = dscale[c]
    for k in range(4):
        out_quats_ref[k : k + 1, :] = dquat[k]
    out_logits_ref[...] = over_cameras(grads[8]) * opacity * (1.0 - opacity)
    sent_one()
    sent_two()
    sent_three()
    sent_four()


def place_kernel(*refs):
    *arrays, sems = refs
    count = len(arrays) // 2
    moves = [
        pltpu.make_async_copy(arrays[k], arrays[count + k], sems.at[k]) for k in range(count)
    ]
    for move in moves:
        move.start()
    for move in moves:
        move.wait()


def per_device(
    centers,
    log_scales,
    quaternions,
    logits,
    harmonics,
    cameras,
    tile_lists,
    tile_counts,
    tile_ids,
    send_index,
    pixel_grad,
):
    n_img, n_view = lax.axis_size("img"), lax.axis_size("view")
    tiles = tile_ids.shape[2]
    sizes = (16.0 * TW, 8.0 * TW, 8.0 * (n_img * tiles // TW))
    vmem, hbm = pl.BlockSpec(memory_space=pltpu.VMEM), pl.BlockSpec(memory_space=pltpu.HBM)
    per_view, per_img = (n_view, ROWS, LANES), (n_img, ROWS, LANES)
    inputs = (
        cameras.T,
        centers,
        log_scales,
        quaternions,
        logits.reshape(1, -1),
        harmonics,
        send_index[0, 0],
        tile_lists[0, 0],
        tile_counts[0, 0],
        tile_ids[0, 0],
        pixel_grad[0, 0].transpose(1, 0, 2),
    )
    shapes = [
        jax.ShapeDtypeStruct((3, tiles, PIX), F32),
        jax.ShapeDtypeStruct((3, LANES), F32),
        jax.ShapeDtypeStruct((3, LANES), F32),
        jax.ShapeDtypeStruct((4, LANES), F32),
        jax.ShapeDtypeStruct((1, LANES), F32),
        jax.ShapeDtypeStruct((48, LANES), F32),
    ]
    results = pl.pallas_call(
        functools.partial(train_kernel, n_img, n_view, sizes),
        out_shape=shapes,
        in_specs=[hbm] * len(inputs),
        out_specs=[vmem] * len(shapes),
        scratch_shapes=[
            pltpu.VMEM(per_view, F32),
            pltpu.VMEM(per_view, F32),
            pltpu.VMEM(per_img, F32),
            pltpu.VMEM(per_img, F32),
            pltpu.VMEM((n_img // 2, 2, ROWS, LANES), F32),
            pltpu.VMEM(per_img, F32),
            pltpu.VMEM((n_view // 2, 2, ROWS, LANES), F32),
            pltpu.VMEM(per_view, F32),
        ]
        + [
            (pltpu.SMEM if value.shape == (tiles,) else pltpu.VMEM)(value.shape, value.dtype)
            for value in inputs
        ]
        + [
            pltpu.VMEM((2, n_view // 2, 32, LANES), BF16),
            pltpu.VMEM((2, n_img // 2, 32, LANES), BF16),
            pltpu.VMEM((256, n_img * LANES), BF16),
            pltpu.VMEM((256, tiles * PIX), BF16),
            pltpu.SemaphoreType.DMA((4, n_view)),
            pltpu.SemaphoreType.DMA((4, n_img)),
            pltpu.SemaphoreType.DMA((len(inputs),)),
        ],
        compiler_params=pltpu.CompilerParams(
            collective_id=0, has_side_effects=True, vmem_limit_bytes=63 * 1024 * 1024
        ),
    )(*inputs)
    out = pl.pallas_call(
        place_kernel,
        out_shape=shapes,
        in_specs=[vmem] * len(shapes),
        out_specs=[hbm] * len(shapes),
        scratch_shapes=[pltpu.SemaphoreType.DMA((len(shapes),))],
    )(*results)
    picture = out[0].transpose(1, 0, 2)[None, None]
    return (picture, out[1], out[2], out[3], out[4].reshape(-1), out[5])


def solution(mesh):
    split = P(None, ("img", "view"))
    placed = (
        split,
        split,
        split,
        P(("img", "view")),
        split,
        P(),
        P("view", "img", None, None),
        P("view", "img", None),
        P("view", "img", None),
        P("view", "img", None, None),
        P("view", "img", None, None, None),
    )
    return jax.shard_map(
        per_device,
        mesh=mesh,
        in_specs=placed,
        out_specs=(P("view", "img", None, None, None), split, split, split, P(("img", "view")), split),
        check_vma=False,
    )
```

```python
import functools

import jax
import jax.numpy as jnp
from jax import lax
from jax.experimental import pallas as pl
from jax.experimental.pallas import tpu as pltpu
from jax.sharding import PartitionSpec as P

TW = 8
ROWS = 9
LANES = 128
PIX = 256
MINOR = {"view": 4, "img": 2}
LINES = 16
FINE_ROWS = (2, 3, 4)
LOG2E = 1.4426950408889634
CAMERA_DISTANCE = 4.0
C0 = 0.28209479177387814
C1 = 0.4886025119029199
C20, C21, C22, C23, C24 = (
    1.0925484305920792,
    -1.0925484305920792,
    0.31539156525252005,
    -1.0925484305920792,
    0.5462742152960396,
)
C30, C31, C32, C33, C34, C35, C36 = (
    -0.5900435899266435,
    2.890611442640554,
    -0.4570457994644658,
    0.3731763325901154,
    -0.4570457994644658,
    1.445305721320277,
    -0.5900435899266435,
)
F32 = jnp.float32
BF16 = jnp.bfloat16


def split_two(value):
    high = value.astype(BF16)
    low = (value - high.astype(F32)).astype(BF16)
    return high, low


def dot(left, right):
    return lax.dot_general(left, right, (((1,), (0,)), ((), ())), preferred_element_type=F32)


def dot_nt(left, right):
    return lax.dot_general(left, right, (((1,), (1,)), ((), ())), preferred_element_type=F32)


def rotations(cameras, count):
    turns = jnp.concatenate([jnp.cos(cameras), jnp.sin(cameras)], axis=0).T
    ca, cb, cg, sa, sb, sg = (
        jnp.broadcast_to(turns[:, k : k + 1], (count, LANES)) for k in range(6)
    )
    return [
        [cg * ca, cg * sa * sb - sg * cb, cg * sa * cb + sg * sb],
        [sg * ca, sg * sa * sb + cg * cb, sg * sa * cb - cg * sb],
        [-sa, ca * sb, ca * cb],
    ]


def shape_factor(quats, scales):
    inv = lax.rsqrt(sum(q * q for q in quats))
    w, x, y, z = (q * inv for q in quats)
    rot = [
        [1.0 - 2.0 * (y * y + z * z), 2.0 * (x * y - w * z), 2.0 * (x * z + w * y)],
        [2.0 * (x * y + w * z), 1.0 - 2.0 * (x * x + z * z), 2.0 * (y * z - w * x)],
        [2.0 * (x * z - w * y), 2.0 * (y * z + w * x), 1.0 - 2.0 * (x * x + y * y)],
    ]
    stretch = [jnp.exp(s) for s in scales]
    factor = [[rot[r][k] * stretch[k] for k in range(3)] for r in range(3)]
    return (w, x, y, z), inv, stretch, factor


def basis_of(x, y, z):
    xx, yy, zz = x * x, y * y, z * z
    return [
        None,
        -C1 * y,
        C1 * z,
        -C1 * x,
        C20 * x * y,
        C21 * y * z,
        C22 * (2.0 * zz - xx - yy),
        C23 * x * z,
        C24 * (xx - yy),
        C30 * y * (3.0 * xx - yy),
        C31 * x * y * z,
        C32 * y * (4.0 * zz - xx - yy),
        C33 * z * (2.0 * zz - 3.0 * xx - 3.0 * yy),
        C34 * x * (4.0 * zz - xx - yy),
        C35 * z * (xx - yy),
        C36 * x * (xx - 3.0 * yy),
    ]


def project(rot, centers, factor, harm_ref, focal, half_w, half_h):
    pts = [rot[r][0] * centers[0] + rot[r][1] * centers[1] + rot[r][2] * centers[2] for r in range(3)]
    iz = 1.0 / (pts[2] + CAMERA_DISTANCE)
    fiz = focal * iz
    tx, ty = pts[0] * iz, pts[1] * iz
    t0 = [fiz * (rot[0][c] - tx * rot[2][c]) for c in range(3)]
    t1 = [fiz * (rot[1][c] - ty * rot[2][c]) for c in range(3)]
    s0 = [t0[0] * factor[0][k] + t0[1] * factor[1][k] + t0[2] * factor[2][k] for k in range(3)]
    s1 = [t1[0] * factor[0][k] + t1[1] * factor[1][k] + t1[2] * factor[2][k] for k in range(3)]
    cov_a = s0[0] * s0[0] + s0[1] * s0[1] + s0[2] * s0[2] + 0.3
    cov_b = s0[0] * s1[0] + s0[1] * s1[1] + s0[2] * s1[2]
    cov_c = s1[0] * s1[0] + s1[1] * s1[1] + s1[2] * s1[2] + 0.3
    inv_det = 1.0 / (cov_a * cov_c - cov_b * cov_b)
    conic = (cov_c * inv_det, -cov_b * inv_det, cov_a * inv_det)
    offs = [centers[c] + CAMERA_DISTANCE * rot[2][c] for c in range(3)]
    inv_len = lax.rsqrt(offs[0] * offs[0] + offs[1] * offs[1] + offs[2] * offs[2])
    x, y, z = (o * inv_len for o in offs)
    basis = basis_of(x, y, z)
    shade = []
    for ch in range(3):
        total = 0.5 + C0 * harm_ref[ch : ch + 1, :]
        for l in range(1, 16):
            total = total + basis[l] * harm_ref[3 * l + ch : 3 * l + ch + 1, :]
        shade.append(total)
    colour = [jnp.maximum(s, 0.0) for s in shade]
    values = [focal * tx + half_w, focal * ty + half_h, *conic, *colour]
    saved = (iz, fiz, tx, ty, t0, t1, s0, s1, conic, inv_det, inv_len, (x, y, z), basis, shade)
    return values, saved


def over_cameras(value):
    return jnp.sum(value, axis=0, keepdims=True)


def project_back(rot, factor, harm_ref, focal, saved, grads, grad_harm_ref):
    iz, fiz, tx, ty, t0, t1, s0, s1, conic, inv_det, inv_len, (x, y, z), basis, shade = saved
    du, dv, dca, dcb, dcc = grads[:5]
    dcol = []
    for ch in range(3):
        g = grads[5 + ch]
        dcol.append(jnp.where(shade[ch] > 0.0, g, jnp.where(shade[ch] == 0.0, 0.5 * g, 0.0)))
    e = [None]
    for ch in range(3):
        grad_harm_ref[ch : ch + 1, :] = C0 * over_cameras(dcol[ch])
    for l in range(1, 16):
        e.append(sum(harm_ref[3 * l + ch : 3 * l + ch + 1, :] * dcol[ch] for ch in range(3)))
        for ch in range(3):
            grad_harm_ref[3 * l + ch : 3 * l + ch + 1, :] = over_cameras(basis[l] * dcol[ch])
    xx, yy, zz, xy, yz, xz = x * x, y * y, z * z, x * y, y * z, x * z
    dx = (
        -C1 * e[3]
        + C20 * y * e[4]
        + x * (2.0 * C24 * e[8] - 2.0 * C22 * e[6])
        + C23 * z * e[7]
        + xy * (6.0 * C30 * e[9] - 2.0 * C32 * e[11])
        + C31 * yz * e[10]
        + xz * (2.0 * C35 * e[14] - 6.0 * C33 * e[12])
        + C34 * (4.0 * zz - 3.0 * xx - yy) * e[13]
        + 3.0 * C36 * (xx - yy) * e[15]
    )
    dy = (
        -C1 * e[1]
        + C20 * x * e[4]
        + C21 * z * e[5]
        - y * (2.0 * C22 * e[6] + 2.0 * C24 * e[8])
        + 3.0 * C30 * (xx - yy) * e[9]
        + C31 * xz * e[10]
        + C32 * (4.0 * zz - xx - 3.0 * yy) * e[11]
        - yz * (6.0 * C33 * e[12] + 2.0 * C35 * e[14])
        - xy * (2.0 * C34 * e[13] + 6.0 * C36 * e[15])
    )
    dz = (
        C1 * e[2]
        + C21 * y * e[5]
        + 4.0 * C22 * z * e[6]
        + C23 * x * e[7]
        + C31 * xy * e[10]
        + 8.0 * C32 * yz * e[11]
        + C33 * (6.0 * zz - 3.0 * xx - 3.0 * yy) * e[12]
        + 8.0 * C34 * xz * e[13]
        + C35 * (xx - yy) * e[14]
    )
    along = x * dx + y * dy + z * dz
    doff = [inv_len * (dx - x * along), inv_len * (dy - y * along), inv_len * (dz - z * along)]
    ca, cb, cc = conic
    s = dca * ca + dcb * cb + dcc * cc
    da = inv_det * dcc - s * ca
    dc = inv_det * dca - s * cc
    db = -(inv_det * dcb) - 2.0 * s * cb
    da2, dc2 = da + da, dc + dc
    ds0 = [da2 * s0[k] + db * s1[k] for k in range(3)]
    ds1 = [dc2 * s1[k] + db * s0[k] for k in range(3)]
    dt0 = [sum(ds0[k] * factor[c][k] for k in range(3)) for c in range(3)]
    dt1 = [sum(ds1[k] * factor[c][k] for k in range(3)) for c in range(3)]
    dfactor = [[over_cameras(t0[c] * ds0[k] + t1[c] * ds1[k]) for k in range(3)] for c in range(3)]
    n0 = sum(dt0[c] * rot[2][c] for c in range(3))
    n1 = sum(dt1[c] * rot[2][c] for c in range(3))
    m0 = sum(dt0[c] * rot[0][c] for c in range(3))
    m1 = sum(dt1[c] * rot[1][c] for c in range(3))
    dfiz = (m0 - tx * n0) + (m1 - ty * n1)
    dtx = focal * du - fiz * n0
    dty = focal * dv - fiz * n1
    dp = [dtx * iz, dty * iz, -iz * (fiz * dfiz + dtx * tx + dty * ty)]
    dcenters = [
        over_cameras(sum(rot[r][c] * dp[r] for r in range(3)) + doff[c]) for c in range(3)
    ]
    return dcenters, dfactor


def shape_back(unit, inv, stretch, factor, dfactor):
    w, x, y, z = unit
    dscale = [sum(factor[r][k] * dfactor[r][k] for r in range(3)) for k in range(3)]
    d = [[dfactor[r][k] * stretch[k] for k in range(3)] for r in range(3)]
    dw = 2.0 * (z * (d[1][0] - d[0][1]) + y * (d[0][2] - d[2][0]) + x * (d[2][1] - d[1][2]))
    dx = 2.0 * (
        y * (d[0][1] + d[1][0]) + z * (d[0][2] + d[2][0]) + w * (d[2][1] - d[1][2])
    ) - 4.0 * x * (d[1][1] + d[2][2])
    dy = 2.0 * (
        x * (d[0][1] + d[1][0]) + z * (d[1][2] + d[2][1]) + w * (d[0][2] - d[2][0])
    ) - 4.0 * y * (d[0][0] + d[2][2])
    dz = 2.0 * (
        x * (d[0][2] + d[2][0]) + y * (d[1][2] + d[2][1]) + w * (d[1][0] - d[0][1])
    ) - 4.0 * z * (d[0][0] + d[1][1])
    along = w * dw + x * dx + y * dy + z * dz
    dquat = [inv * (g - q * along) for g, q in zip((dw, dx, dy, dz), unit)]
    return dscale, dquat


def lane_pick(table, lanes):
    return jnp.take_along_axis(table, lanes, axis=1, mode="promise_in_bounds")


def triangle(later):
    row = lax.broadcasted_iota(jnp.int32, (PIX, PIX), 0)
    col = lax.broadcasted_iota(jnp.int32, (PIX, PIX), 1)
    return jnp.where(row > col if later else row < col, 1.0, 0.0).astype(BF16)


class Tile:
    def __init__(self, geometry, opacity, count, number, grad, grad_t):
        entry = lax.broadcasted_iota(jnp.int32, (1, PIX), 1)
        self.live = jnp.where(entry < count, opacity, 0.0)
        self.opacity = opacity
        left = (16 * lax.rem(number, TW) + 8).astype(F32)
        top = (16 * lax.div(number, TW) + 8).astype(F32)
        self.u, self.v = geometry[0:1] - left, geometry[1:2] - top
        self.conic = geometry[2:3], geometry[3:4], geometry[4:5]
        ca, cb, cc = self.conic
        self.local = lax.broadcasted_iota(jnp.int32, (16, PIX), 0).astype(F32) - 7.5
        dx, self.dy = self.local - self.u, self.local - self.v
        self.part_a = (-0.5 * LOG2E * ca) * dx * dx
        self.part_b = (-LOG2E * cb) * dx
        self.part_c = (-0.5 * LOG2E * cc) * self.dy * self.dy
        self.colour = split_two(geometry[5:8])
        self.grad, self.grad_t = grad, grad_t
        c_hi, c_lo = self.colour
        self.mix = jnp.concatenate([c_hi, c_lo, c_hi], axis=0)
        self.moments = [None, None, None]
        self.weights = []

    def shade(self, at, before):
        alphas = []
        for line in range(at, at + LINES):
            power = self.part_a + self.part_b * self.dy[line : line + 1] + self.part_c[line : line + 1]
            alphas.append(self.live * jnp.exp2(power))
        alpha = jnp.concatenate(alphas, axis=0)
        log_left = jnp.log2(1.0 - alpha)
        log_hi, log_lo = split_two(log_left)
        reach = dot(self.grad_t[16 * at : 16 * (at + LINES)], self.mix)
        return at, alpha, log_left, dot(log_hi, before) + dot(log_lo, before), reach

    def weigh(self, shaded, after):
        at, alpha, log_left, log_trans, reach = shaded
        weight = alpha * jnp.exp2(log_trans)
        gain = weight * reach
        g_hi, g_lo = split_two(gain)
        self.weights.append(split_two(weight))
        return at, alpha, log_left, gain, dot(g_hi, after) + dot(g_lo, after)

    def collect(self, weighed):
        at, alpha, log_left, gain, behind = weighed
        back = gain - behind * (alpha * jnp.exp2(-log_left))
        for k in range(LINES):
            piece = back[16 * k : 16 * k + 16]
            level = at + k - 7.5
            terms = (piece, level * piece, (level * level) * piece)
            for m in range(3):
                self.moments[m] = terms[m] if self.moments[m] is None else self.moments[m] + terms[m]

    def finish(self):
        w_hi = jnp.concatenate([w[0] for w in self.weights], axis=0)
        w_lo = jnp.concatenate([w[1] for w in self.weights], axis=0)
        c_hi, c_lo = self.colour
        first = dot_nt(jnp.concatenate([c_hi, c_lo], axis=0), w_hi)
        picture = first[0:3] + first[3:6] + dot_nt(c_hi, w_lo)
        g_hi, g_lo = split_two(self.grad)
        first = dot(jnp.concatenate([g_hi, g_lo], axis=0), w_hi)
        dcolour = first[0:3] + first[3:6] + dot(g_hi, w_lo)

        def total(value):
            return jnp.sum(value, axis=0, keepdims=True)

        u, v, (ca, cb, cc), local = self.u, self.v, self.conic, self.local
        m0, my, myy = (total(m) for m in self.moments)
        mx, mxy = total(local * self.moments[0]), total(local * self.moments[1])
        mxx = total(local * local * self.moments[0])
        qx, qy = mx - u * m0, my - v * m0
        qxx = mxx - u * (mx + qx)
        qyy = myy - v * (my + qy)
        qxy = mxy - u * my - v * qx
        grads = [
            ca * qx + cb * qy,
            cb * qx + cc * qy,
            -0.5 * qxx,
            -qxy,
            -0.5 * qyy,
            dcolour[0:1],
            dcolour[1:2],
            dcolour[2:3],
            m0 / self.opacity,
        ]
        return picture, grads


def render(tiles, before, after):
    parts = [(tile, at) for tile in tiles for at in range(0, 16, LINES)]
    shaded, weighed, done = [], [], []
    for step in range(len(parts) + 2):
        if step >= 2:
            tile, at = parts[step - 2]
            tile.collect(weighed[step - 2])
            weighed[step - 2] = None
            if at + LINES == 16:
                done.append(tile.finish())
        if 1 <= step <= len(parts):
            weighed.append(parts[step - 1][0].weigh(shaded[step - 1], after))
            shaded[step - 1] = None
        if step < len(parts):
            shaded.append(parts[step][0].shade(parts[step][1], before))
    return done


def ring(size, steps):
    return min(steps, size - steps)


def farthest_first(axis, size):
    minor = MINOR[axis]
    major = size // minor
    offsets = [(a, b) for a in range(major) for b in range(minor) if a or b]
    return sorted(offsets, key=lambda o: -ring(major, o[0]) - ring(minor, o[1]) * (axis == "view"))


def neighbour(me, offset, axis, size):
    minor = MINOR[axis]
    major = size // minor

    def wrap(value, limit):
        return jnp.where(value >= limit, value - limit, value)

    return wrap(lax.div(me, minor) + offset[0], major) * minor + wrap(
        lax.rem(me, minor) + offset[1], minor
    )


def exchange(axis, me, size, source, landing, send_sem, recv_sem):
    peers = [neighbour(me, offset, axis, size) for offset in farthest_first(axis, size)]

    def copy(peer, slot):
        return pltpu.make_async_remote_copy(
            src_ref=source(peer),
            dst_ref=landing.at[slot],
            send_sem=send_sem.at[peer],
            recv_sem=recv_sem.at[slot],
            device_id={axis: peer},
            device_id_type=pl.DeviceIdType.MESH,
        )

    for peer in peers:
        copy(peer, me).start()

    def arrived(peer):
        copy(peer, peer).wait_recv()

    def sent():
        for peer in peers:
            copy(peer, me).wait_send()

    return peers[::-1], arrived, sent


def greet(axis, me, size, barrier):
    for offset in farthest_first(axis, size):
        pl.semaphore_signal(
            barrier,
            inc=1,
            device_id={axis: neighbour(me, offset, axis, size)},
            device_id_type=pl.DeviceIdType.MESH,
        )


def split_rows(block):
    parts, lasts = [], []
    front, last = block[0:8], block[8:9]
    for _ in range(3):
        parts.append(front.astype(BF16).astype(F32))
        lasts.append(last.astype(BF16).astype(F32))
        front, last = front - parts[-1], last - lasts[-1]
    filler = jnp.zeros((5, LANES), F32)
    return jnp.concatenate(parts + lasts + [filler], axis=0).astype(BF16)


def by_distance(axis, size, cuts):
    major = size // MINOR[axis]
    return [
        [a for a in range(major) if low < ring(major, a) <= high]
        for low, high in zip((-1, *cuts), (*cuts, major))
    ]


def pick(axis, me, size, cuts, arrived, landing, high, hot):
    minor = MINOR[axis]
    total = None
    for group in by_distance(axis, size, cuts):
        numbers = []
        for a in group:
            for b in range(minor):
                if a or b:
                    arrived(neighbour(me, (a, b), axis, size))
            first = lax.div(neighbour(me, (a, 0), axis, size), minor) * (minor // 2)
            numbers += [first + k for k in range(minor // 2)]
        table = [
            jnp.concatenate([split_rows(landing[2 * n]), split_rows(landing[2 * n + 1])], axis=1)
            for n in numbers
        ]
        found = dot(jnp.concatenate(table, axis=0), hot)
        for k, n in enumerate(numbers):
            part = jnp.where(high == n, found[32 * k : 32 * k + 32], 0.0)
            total = part if total is None else total + part
    return total[0:8] + total[8:16] + total[16:24], total[24:25] + total[25:26] + total[26:27]


def scatter_sides(index, groups):
    count = index.shape[1]
    high, low = lax.shift_right_logical(index, 8), lax.bitwise_and(index, 255)
    mask = lax.broadcasted_iota(jnp.int32, (groups, count), 0) == high
    hot = lax.broadcasted_iota(jnp.int32, (256, count), 0) == low
    return high, mask, jnp.where(hot, 1.0, 0.0).astype(BF16)


def scatter(rows, mask, hot):
    return scattered(scatter_parts(rows, mask, hot), mask.shape[0], len(rows))


def scatter_parts(rows, mask, hot):
    sides = []
    for r, row in enumerate(rows):
        for _ in range(parts_of(r)):
            high = row.astype(BF16).astype(F32)
            sides.append(jnp.where(mask, high, 0.0))
            row = row - high
    if len(sides) * mask.shape[0] % 16:
        sides.append(jnp.zeros_like(sides[0]))
    return dot_nt(jnp.concatenate(sides, axis=0).astype(BF16), hot)


def parts_of(row):
    return 3 if row in FINE_ROWS else 2


def scattered(out, groups, count):
    sums, at = [], 0
    for r in range(count):
        sums.append(sum(out[groups * k : groups * (k + 1)] for k in range(at, at + parts_of(r))))
        at += parts_of(r)
    return sums


def train_kernel(
    n_img,
    n_view,
    sizes,
    cameras_in,
    centers_in,
    scales_in,
    quats_in,
    logits_in,
    harm_in,
    slots_in,
    lists_in,
    counts_in,
    ids_in,
    grad_in,
    picture_ref,
    out_centers_ref,
    out_scales_ref,
    out_quats_ref,
    out_logits_ref,
    out_harm_ref,
    send_one,
    recv_one,
    send_two,
    recv_two,
    send_three,
    recv_three,
    send_four,
    recv_four,
    cameras_ref,
    centers_ref,
    scales_ref,
    quats_ref,
    logits_ref,
    harm_ref,
    slots_ref,
    lists_ref,
    counts_ref,
    ids_ref,
    grad_ref,
    slot_hot,
    entry_hot,
    view_sems,
    img_sems,
    load_sems,
):
    focal, half_w, half_h = sizes
    img, view = lax.axis_index("img"), lax.axis_index("view")
    barrier = pltpu.get_barrier_semaphore()
    loads = [
        pltpu.make_async_copy(source, target, load_sems.at[k])
        for k, (source, target) in enumerate(
            (
                (cameras_in, cameras_ref),
                (centers_in, centers_ref),
                (scales_in, scales_ref),
                (quats_in, quats_ref),
                (logits_in, logits_ref),
                (harm_in, harm_ref),
                (slots_in, slots_ref),
                (lists_in, lists_ref),
                (counts_in, counts_ref),
                (ids_in, ids_ref),
                (grad_in, grad_ref),
            )
        )
    ]
    for load in loads[:6]:
        load.start()
    greet("view", view, n_view, barrier)
    greet("img", img, n_img, barrier)
    for load in loads[6:]:
        load.start()
    for load in loads[:6]:
        load.wait()

    rot = rotations(cameras_ref[...], n_view)
    centers = [centers_ref[c : c + 1, :] for c in range(3)]
    unit, inv_norm, stretch, factor = shape_factor(
        [quats_ref[k : k + 1, :] for k in range(4)], [scales_ref[k : k + 1, :] for k in range(3)]
    )
    opacity = 1.0 / (1.0 + jnp.exp(-logits_ref[...]))
    values, saved = project(rot, centers, factor, harm_ref, focal, half_w, half_h)
    for r, value in enumerate(values):
        send_one[:, r, :] = value
    send_one[:, 8, :] = jnp.broadcast_to(opacity, (n_view, LANES))

    for load in loads[6:]:
        load.wait()
    pl.semaphore_wait(barrier, n_view + n_img - 2)
    peers, arrived, sent_one = exchange(
        "view", view, n_view, lambda p: send_one.at[p], recv_one, view_sems.at[0], view_sems.at[1]
    )

    slot_index = jnp.concatenate([slots_ref[d : d + 1, :] for d in range(n_img)], axis=1)
    slot_high, _, hot = scatter_sides(slot_index, n_view // 2)
    for d in range(n_img):
        slot_hot[d] = hot[:, LANES * d : LANES * d + LANES]
    recv_one[view] = send_one[view]
    geometry, last = pick("view", view, n_view, (1, 3), arrived, recv_one, slot_high, hot)
    for d in range(n_img):
        send_two[d, 0:8, :] = geometry[:, LANES * d : LANES * d + LANES]
        send_two[d, 8:9, :] = last[:, LANES * d : LANES * d + LANES]

    peers, arrived, sent_two = exchange(
        "img", img, n_img, lambda p: send_two.at[p], recv_two, img_sems.at[0], img_sems.at[1]
    )

    tiles = lists_ref.shape[0]
    lists = lists_ref[...]
    entry_index = jnp.concatenate([lists[t : t + 1] for t in range(tiles)], axis=1)
    entry_high, entry_mask, hot = scatter_sides(entry_index, n_img // 2)
    entry_hot[...] = hot
    before, after = triangle(False), triangle(True)
    recv_two[img] = send_two[img]
    geometry, last = pick("img", img, n_img, (3,), arrived, recv_two, entry_high, hot)
    work = []
    for t in range(tiles):
        grad = grad_ref[:, t, :]
        high = grad.astype(BF16).astype(F32)
        grad_t = jnp.concatenate([high, high, grad - high], axis=0).T.astype(BF16)
        at = slice(PIX * t, PIX * t + PIX)
        work.append(Tile(geometry[:, at], last[:, at], counts_ref[t], ids_ref[t], grad, grad_t))
    rendered = render(work, before, after)
    for t in range(tiles):
        picture_ref[:, t, :] = rendered[t][0]

    rows = [jnp.concatenate([grads[r] for _, grads in rendered], axis=1) for r in range(ROWS)]
    for r, total in enumerate(scatter(rows, entry_mask, entry_hot[...])):
        for h in range(2):
            send_three[:, h, r, :] = total[:, LANES * h : LANES * h + LANES]
    peers, arrived, sent_three = exchange(
        "img",
        img,
        n_img,
        lambda p: send_three.at[lax.div(p, 2), lax.rem(p, 2)],
        recv_three,
        img_sems.at[2],
        img_sems.at[3],
    )
    recv_three[img] = send_three[lax.div(img, 2), lax.rem(img, 2)]
    out = None
    for group in by_distance("img", n_img, (1, 3)):
        places = []
        for a in group:
            for b in range(MINOR["img"]):
                places.append(neighbour(img, (a, b), "img", n_img))
                if a or b:
                    arrived(places[-1])
        rows = [
            jnp.concatenate([recv_three[p, r : r + 1, :] for p in places], axis=1) for r in range(ROWS)
        ]
        high = lax.shift_right_logical(
            jnp.concatenate([slots_ref[pl.ds(p, 1), :] for p in places], axis=1), 8
        )
        mask = lax.broadcasted_iota(jnp.int32, (n_view // 2, high.shape[1]), 0) == high
        part = scatter_parts(rows, mask, jnp.concatenate([slot_hot[p] for p in places], axis=1))
        out = part if out is None else out + part
    for r, total in enumerate(scattered(out, n_view // 2, ROWS)):
        for h in range(2):
            send_four[:, h, r, :] = total[:, LANES * h : LANES * h + LANES]
    peers, arrived, sent_four = exchange(
        "view",
        view,
        n_view,
        lambda p: send_four.at[lax.div(p, 2), lax.rem(p, 2)],
        recv_four,
        view_sems.at[2],
        view_sems.at[3],
    )
    recv_four[view] = send_four[lax.div(view, 2), lax.rem(view, 2)]

    for peer in peers:
        arrived(peer)

    grads = [recv_four[:, r, :] for r in range(ROWS)]
    dcenters, dfactor = project_back(rot, factor, harm_ref, focal, saved, grads, out_harm_ref)
    dscale, dquat = shape_back(unit, inv_norm, stretch, factor, dfactor)
    for c in range(3):
        out_centers_ref[c : c + 1, :] = dcenters[c]
        out_scales_ref[c : c + 1, :] = dscale[c]
    for k in range(4):
        out_quats_ref[k : k + 1, :] = dquat[k]
    out_logits_ref[...] = over_cameras(grads[8]) * opacity * (1.0 - opacity)
    sent_one()
    sent_two()
    sent_three()
    sent_four()


def place_kernel(*refs):
    *arrays, sems = refs
    count = len(arrays) // 2
    moves = [
        pltpu.make_async_copy(arrays[k], arrays[count + k], sems.at[k]) for k in range(count)
    ]
    for move in moves:
        move.start()
    for move in moves:
        move.wait()


def per_device(
    centers,
    log_scales,
    quaternions,
    logits,
    harmonics,
    cameras,
    tile_lists,
    tile_counts,
    tile_ids,
    send_index,
    pixel_grad,
):
    n_img, n_view = lax.axis_size("img"), lax.axis_size("view")
    tiles = tile_ids.shape[2]
    sizes = (16.0 * TW, 8.0 * TW, 8.0 * (n_img * tiles // TW))
    vmem, hbm = pl.BlockSpec(memory_space=pltpu.VMEM), pl.BlockSpec(memory_space=pltpu.HBM)
    per_view, per_img = (n_view, ROWS, LANES), (n_img, ROWS, LANES)
    inputs = (
        cameras.T,
        centers,
        log_scales,
        quaternions,
        logits.reshape(1, -1),
        harmonics,
        send_index[0, 0],
        tile_lists[0, 0],
        tile_counts[0, 0],
        tile_ids[0, 0],
        pixel_grad[0, 0].transpose(1, 0, 2),
    )
    shapes = [
        jax.ShapeDtypeStruct((3, tiles, PIX), F32),
        jax.ShapeDtypeStruct((3, LANES), F32),
        jax.ShapeDtypeStruct((3, LANES), F32),
        jax.ShapeDtypeStruct((4, LANES), F32),
        jax.ShapeDtypeStruct((1, LANES), F32),
        jax.ShapeDtypeStruct((48, LANES), F32),
    ]
    results = pl.pallas_call(
        functools.partial(train_kernel, n_img, n_view, sizes),
        out_shape=[pltpu.VMEM(shape.shape, shape.dtype) for shape in shapes],
        in_specs=[hbm] * len(inputs),
        out_specs=[vmem] * len(shapes),
        scratch_shapes=[
            pltpu.VMEM(per_view, F32),
            pltpu.VMEM(per_view, F32),
            pltpu.VMEM(per_img, F32),
            pltpu.VMEM(per_img, F32),
            pltpu.VMEM((n_img // 2, 2, ROWS, LANES), F32),
            pltpu.VMEM(per_img, F32),
            pltpu.VMEM((n_view // 2, 2, ROWS, LANES), F32),
            pltpu.VMEM(per_view, F32),
        ]
        + [
            (pltpu.SMEM if value.shape == (tiles,) else pltpu.VMEM)(value.shape, value.dtype)
            for value in inputs
        ]
        + [
            pltpu.VMEM((n_img, 256, LANES), BF16),
            pltpu.VMEM((256, tiles * PIX), BF16),
            pltpu.SemaphoreType.DMA((4, n_view)),
            pltpu.SemaphoreType.DMA((4, n_img)),
            pltpu.SemaphoreType.DMA((len(inputs),)),
        ],
        compiler_params=pltpu.CompilerParams(
            collective_id=0, has_side_effects=True, vmem_limit_bytes=63 * 1024 * 1024
        ),
    )(*inputs)
    out = pl.pallas_call(
        place_kernel,
        out_shape=shapes,
        in_specs=[vmem] * len(shapes),
        out_specs=[hbm] * len(shapes),
        scratch_shapes=[pltpu.SemaphoreType.DMA((len(shapes),))],
    )(*(pltpu.with_memory_space_constraint(value, pltpu.VMEM) for value in results))
    picture = out[0].transpose(1, 0, 2)[None, None]
    return (picture, out[1], out[2], out[3], out[4].reshape(-1), out[5])


def solution(mesh):
    split = P(None, ("img", "view"))
    placed = (
        split,
        split,
        split,
        P(("img", "view")),
        split,
        P(),
        P("view", "img", None, None),
        P("view", "img", None),
        P("view", "img", None),
        P("view", "img", None, None),
        P("view", "img", None, None, None),
    )
    return jax.shard_map(
        per_device,
        mesh=mesh,
        in_specs=placed,
        out_specs=(P("view", "img", None, None, None), split, split, split, P(("img", "view")), split),
        check_vma=False,
    )
```

```python
import functools

import jax
import jax.numpy as jnp
from jax import lax
from jax.experimental import pallas as pl
from jax.experimental.pallas import tpu as pltpu
from jax.sharding import PartitionSpec as P

TW = 8
ROWS = 9
LANES = 128
PIX = 256
MINOR = {"view": 4, "img": 2}
LINES = 16
FINE_ROWS = (2, 3, 4)
LOG2E = 1.4426950408889634
CAMERA_DISTANCE = 4.0
C0 = 0.28209479177387814
C1 = 0.4886025119029199
C20, C21, C22, C23, C24 = (
    1.0925484305920792,
    -1.0925484305920792,
    0.31539156525252005,
    -1.0925484305920792,
    0.5462742152960396,
)
C30, C31, C32, C33, C34, C35, C36 = (
    -0.5900435899266435,
    2.890611442640554,
    -0.4570457994644658,
    0.3731763325901154,
    -0.4570457994644658,
    1.445305721320277,
    -0.5900435899266435,
)
F32 = jnp.float32
BF16 = jnp.bfloat16


def split_two(value):
    high = value.astype(BF16)
    low = (value - high.astype(F32)).astype(BF16)
    return high, low


def dot(left, right):
    return lax.dot_general(left, right, (((1,), (0,)), ((), ())), preferred_element_type=F32)


def dot_nt(left, right):
    return lax.dot_general(left, right, (((1,), (1,)), ((), ())), preferred_element_type=F32)


def rotations(cameras, count):
    turns = jnp.concatenate([jnp.cos(cameras), jnp.sin(cameras)], axis=0).T
    ca, cb, cg, sa, sb, sg = (
        jnp.broadcast_to(turns[:, k : k + 1], (count, LANES)) for k in range(6)
    )
    return [
        [cg * ca, cg * sa * sb - sg * cb, cg * sa * cb + sg * sb],
        [sg * ca, sg * sa * sb + cg * cb, sg * sa * cb - cg * sb],
        [-sa, ca * sb, ca * cb],
    ]


def shape_factor(quats, scales):
    inv = lax.rsqrt(sum(q * q for q in quats))
    w, x, y, z = (q * inv for q in quats)
    rot = [
        [1.0 - 2.0 * (y * y + z * z), 2.0 * (x * y - w * z), 2.0 * (x * z + w * y)],
        [2.0 * (x * y + w * z), 1.0 - 2.0 * (x * x + z * z), 2.0 * (y * z - w * x)],
        [2.0 * (x * z - w * y), 2.0 * (y * z + w * x), 1.0 - 2.0 * (x * x + y * y)],
    ]
    stretch = [jnp.exp(s) for s in scales]
    factor = [[rot[r][k] * stretch[k] for k in range(3)] for r in range(3)]
    return (w, x, y, z), inv, stretch, factor


def basis_of(x, y, z):
    xx, yy, zz = x * x, y * y, z * z
    return [
        None,
        -C1 * y,
        C1 * z,
        -C1 * x,
        C20 * x * y,
        C21 * y * z,
        C22 * (2.0 * zz - xx - yy),
        C23 * x * z,
        C24 * (xx - yy),
        C30 * y * (3.0 * xx - yy),
        C31 * x * y * z,
        C32 * y * (4.0 * zz - xx - yy),
        C33 * z * (2.0 * zz - 3.0 * xx - 3.0 * yy),
        C34 * x * (4.0 * zz - xx - yy),
        C35 * z * (xx - yy),
        C36 * x * (xx - 3.0 * yy),
    ]


def project(rot, centers, factor, harm_ref, focal, half_w, half_h):
    pts = [rot[r][0] * centers[0] + rot[r][1] * centers[1] + rot[r][2] * centers[2] for r in range(3)]
    iz = 1.0 / (pts[2] + CAMERA_DISTANCE)
    fiz = focal * iz
    tx, ty = pts[0] * iz, pts[1] * iz
    t0 = [fiz * (rot[0][c] - tx * rot[2][c]) for c in range(3)]
    t1 = [fiz * (rot[1][c] - ty * rot[2][c]) for c in range(3)]
    s0 = [t0[0] * factor[0][k] + t0[1] * factor[1][k] + t0[2] * factor[2][k] for k in range(3)]
    s1 = [t1[0] * factor[0][k] + t1[1] * factor[1][k] + t1[2] * factor[2][k] for k in range(3)]
    cov_a = s0[0] * s0[0] + s0[1] * s0[1] + s0[2] * s0[2] + 0.3
    cov_b = s0[0] * s1[0] + s0[1] * s1[1] + s0[2] * s1[2]
    cov_c = s1[0] * s1[0] + s1[1] * s1[1] + s1[2] * s1[2] + 0.3
    inv_det = 1.0 / (cov_a * cov_c - cov_b * cov_b)
    conic = (cov_c * inv_det, -cov_b * inv_det, cov_a * inv_det)
    offs = [centers[c] + CAMERA_DISTANCE * rot[2][c] for c in range(3)]
    inv_len = lax.rsqrt(offs[0] * offs[0] + offs[1] * offs[1] + offs[2] * offs[2])
    x, y, z = (o * inv_len for o in offs)
    basis = basis_of(x, y, z)
    shade = []
    for ch in range(3):
        total = 0.5 + C0 * harm_ref[ch : ch + 1, :]
        for l in range(1, 16):
            total = total + basis[l] * harm_ref[3 * l + ch : 3 * l + ch + 1, :]
        shade.append(total)
    colour = [jnp.maximum(s, 0.0) for s in shade]
    values = [focal * tx + half_w, focal * ty + half_h, *conic, *colour]
    saved = (iz, fiz, tx, ty, t0, t1, s0, s1, conic, inv_det, inv_len, (x, y, z), basis, shade)
    return values, saved


def over_cameras(value):
    return jnp.sum(value, axis=0, keepdims=True)


def project_back(rot, factor, harm_ref, focal, saved, grads, grad_harm_ref):
    iz, fiz, tx, ty, t0, t1, s0, s1, conic, inv_det, inv_len, (x, y, z), basis, shade = saved
    du, dv, dca, dcb, dcc = grads[:5]
    dcol = []
    for ch in range(3):
        g = grads[5 + ch]
        dcol.append(jnp.where(shade[ch] > 0.0, g, jnp.where(shade[ch] == 0.0, 0.5 * g, 0.0)))
    e = [None]
    for ch in range(3):
        grad_harm_ref[ch : ch + 1, :] = C0 * over_cameras(dcol[ch])
    for l in range(1, 16):
        e.append(sum(harm_ref[3 * l + ch : 3 * l + ch + 1, :] * dcol[ch] for ch in range(3)))
        for ch in range(3):
            grad_harm_ref[3 * l + ch : 3 * l + ch + 1, :] = over_cameras(basis[l] * dcol[ch])
    xx, yy, zz, xy, yz, xz = x * x, y * y, z * z, x * y, y * z, x * z
    dx = (
        -C1 * e[3]
        + C20 * y * e[4]
        + x * (2.0 * C24 * e[8] - 2.0 * C22 * e[6])
        + C23 * z * e[7]
        + xy * (6.0 * C30 * e[9] - 2.0 * C32 * e[11])
        + C31 * yz * e[10]
        + xz * (2.0 * C35 * e[14] - 6.0 * C33 * e[12])
        + C34 * (4.0 * zz - 3.0 * xx - yy) * e[13]
        + 3.0 * C36 * (xx - yy) * e[15]
    )
    dy = (
        -C1 * e[1]
        + C20 * x * e[4]
        + C21 * z * e[5]
        - y * (2.0 * C22 * e[6] + 2.0 * C24 * e[8])
        + 3.0 * C30 * (xx - yy) * e[9]
        + C31 * xz * e[10]
        + C32 * (4.0 * zz - xx - 3.0 * yy) * e[11]
        - yz * (6.0 * C33 * e[12] + 2.0 * C35 * e[14])
        - xy * (2.0 * C34 * e[13] + 6.0 * C36 * e[15])
    )
    dz = (
        C1 * e[2]
        + C21 * y * e[5]
        + 4.0 * C22 * z * e[6]
        + C23 * x * e[7]
        + C31 * xy * e[10]
        + 8.0 * C32 * yz * e[11]
        + C33 * (6.0 * zz - 3.0 * xx - 3.0 * yy) * e[12]
        + 8.0 * C34 * xz * e[13]
        + C35 * (xx - yy) * e[14]
    )
    along = x * dx + y * dy + z * dz
    doff = [inv_len * (dx - x * along), inv_len * (dy - y * along), inv_len * (dz - z * along)]
    ca, cb, cc = conic
    s = dca * ca + dcb * cb + dcc * cc
    da = inv_det * dcc - s * ca
    dc = inv_det * dca - s * cc
    db = -(inv_det * dcb) - 2.0 * s * cb
    da2, dc2 = da + da, dc + dc
    ds0 = [da2 * s0[k] + db * s1[k] for k in range(3)]
    ds1 = [dc2 * s1[k] + db * s0[k] for k in range(3)]
    dt0 = [sum(ds0[k] * factor[c][k] for k in range(3)) for c in range(3)]
    dt1 = [sum(ds1[k] * factor[c][k] for k in range(3)) for c in range(3)]
    dfactor = [[over_cameras(t0[c] * ds0[k] + t1[c] * ds1[k]) for k in range(3)] for c in range(3)]
    n0 = sum(dt0[c] * rot[2][c] for c in range(3))
    n1 = sum(dt1[c] * rot[2][c] for c in range(3))
    m0 = sum(dt0[c] * rot[0][c] for c in range(3))
    m1 = sum(dt1[c] * rot[1][c] for c in range(3))
    dfiz = (m0 - tx * n0) + (m1 - ty * n1)
    dtx = focal * du - fiz * n0
    dty = focal * dv - fiz * n1
    dp = [dtx * iz, dty * iz, -iz * (fiz * dfiz + dtx * tx + dty * ty)]
    dcenters = [
        over_cameras(sum(rot[r][c] * dp[r] for r in range(3)) + doff[c]) for c in range(3)
    ]
    return dcenters, dfactor


def shape_back(unit, inv, stretch, factor, dfactor):
    w, x, y, z = unit
    dscale = [sum(factor[r][k] * dfactor[r][k] for r in range(3)) for k in range(3)]
    d = [[dfactor[r][k] * stretch[k] for k in range(3)] for r in range(3)]
    dw = 2.0 * (z * (d[1][0] - d[0][1]) + y * (d[0][2] - d[2][0]) + x * (d[2][1] - d[1][2]))
    dx = 2.0 * (
        y * (d[0][1] + d[1][0]) + z * (d[0][2] + d[2][0]) + w * (d[2][1] - d[1][2])
    ) - 4.0 * x * (d[1][1] + d[2][2])
    dy = 2.0 * (
        x * (d[0][1] + d[1][0]) + z * (d[1][2] + d[2][1]) + w * (d[0][2] - d[2][0])
    ) - 4.0 * y * (d[0][0] + d[2][2])
    dz = 2.0 * (
        x * (d[0][2] + d[2][0]) + y * (d[1][2] + d[2][1]) + w * (d[1][0] - d[0][1])
    ) - 4.0 * z * (d[0][0] + d[1][1])
    along = w * dw + x * dx + y * dy + z * dz
    dquat = [inv * (g - q * along) for g, q in zip((dw, dx, dy, dz), unit)]
    return dscale, dquat


def lane_pick(table, lanes):
    return jnp.take_along_axis(table, lanes, axis=1, mode="promise_in_bounds")


def triangle(later):
    row = lax.broadcasted_iota(jnp.int32, (PIX, PIX), 0)
    col = lax.broadcasted_iota(jnp.int32, (PIX, PIX), 1)
    return jnp.where(row > col if later else row < col, 1.0, 0.0).astype(BF16)


class Tile:
    def __init__(self, geometry, opacity, count, number, grad, grad_t):
        entry = lax.broadcasted_iota(jnp.int32, (1, PIX), 1)
        self.live = jnp.where(entry < count, opacity, 0.0)
        self.opacity = opacity
        left = (16 * lax.rem(number, TW) + 8).astype(F32)
        top = (16 * lax.div(number, TW) + 8).astype(F32)
        self.u, self.v = geometry[0:1] - left, geometry[1:2] - top
        self.conic = geometry[2:3], geometry[3:4], geometry[4:5]
        ca, cb, cc = self.conic
        self.local = lax.broadcasted_iota(jnp.int32, (16, PIX), 0).astype(F32) - 7.5
        dx, self.dy = self.local - self.u, self.local - self.v
        self.part_a = (-0.5 * LOG2E * ca) * dx * dx
        self.part_b = (-LOG2E * cb) * dx
        self.part_c = (-0.5 * LOG2E * cc) * self.dy * self.dy
        self.colour = split_two(geometry[5:8])
        self.grad, self.grad_t = grad, grad_t
        c_hi, c_lo = self.colour
        self.mix = jnp.concatenate([c_hi, c_lo, c_hi], axis=0)
        self.moments = [None, None, None]
        self.weights = []

    def shade(self, at, before):
        alphas = []
        for line in range(at, at + LINES):
            power = self.part_a + self.part_b * self.dy[line : line + 1] + self.part_c[line : line + 1]
            alphas.append(self.live * jnp.exp2(power))
        alpha = jnp.concatenate(alphas, axis=0)
        log_left = jnp.log2(1.0 - alpha)
        log_hi, log_lo = split_two(log_left)
        reach = dot(self.grad_t[16 * at : 16 * (at + LINES)], self.mix)
        return at, alpha, log_left, dot(log_hi, before) + dot(log_lo, before), reach

    def weigh(self, shaded, after):
        at, alpha, log_left, log_trans, reach = shaded
        weight = alpha * jnp.exp2(log_trans)
        gain = weight * reach
        g_hi, g_lo = split_two(gain)
        self.weights.append(split_two(weight))
        return at, alpha, log_left, gain, dot(g_hi, after) + dot(g_lo, after)

    def collect(self, weighed):
        at, alpha, log_left, gain, behind = weighed
        back = gain - behind * (alpha * jnp.exp2(-log_left))
        for k in range(LINES):
            piece = back[16 * k : 16 * k + 16]
            level = at + k - 7.5
            terms = (piece, level * piece, (level * level) * piece)
            for m in range(3):
                self.moments[m] = terms[m] if self.moments[m] is None else self.moments[m] + terms[m]

    def finish(self):
        w_hi = jnp.concatenate([w[0] for w in self.weights], axis=0)
        w_lo = jnp.concatenate([w[1] for w in self.weights], axis=0)
        c_hi, c_lo = self.colour
        first = dot_nt(jnp.concatenate([c_hi, c_lo], axis=0), w_hi)
        picture = first[0:3] + first[3:6] + dot_nt(c_hi, w_lo)
        g_hi, g_lo = self.grad
        first = dot(jnp.concatenate([g_hi, g_lo], axis=0), w_hi)
        dcolour = first[0:3] + first[3:6] + dot(g_hi, w_lo)

        def total(value):
            return jnp.sum(value, axis=0, keepdims=True)

        u, v, (ca, cb, cc), local = self.u, self.v, self.conic, self.local
        m0, my, myy = (total(m) for m in self.moments)
        mx, mxy = total(local * self.moments[0]), total(local * self.moments[1])
        mxx = total(local * local * self.moments[0])
        qx, qy = mx - u * m0, my - v * m0
        qxx = mxx - u * (mx + qx)
        qyy = myy - v * (my + qy)
        qxy = mxy - u * my - v * qx
        grads = [
            ca * qx + cb * qy,
            cb * qx + cc * qy,
            -0.5 * qxx,
            -qxy,
            -0.5 * qyy,
            dcolour[0:1],
            dcolour[1:2],
            dcolour[2:3],
            m0 / self.opacity,
        ]
        return picture, grads


def render(tiles, before, after):
    parts = [(tile, at) for tile in tiles for at in range(0, 16, LINES)]
    shaded, weighed, done = [], [], []
    for step in range(len(parts) + 2):
        if step >= 2:
            tile, at = parts[step - 2]
            tile.collect(weighed[step - 2])
            weighed[step - 2] = None
            if at + LINES == 16:
                done.append(tile.finish())
        if 1 <= step <= len(parts):
            weighed.append(parts[step - 1][0].weigh(shaded[step - 1], after))
            shaded[step - 1] = None
        if step < len(parts):
            shaded.append(parts[step][0].shade(parts[step][1], before))
    return done


def ring(size, steps):
    return min(steps, size - steps)


def farthest_first(axis, size):
    minor = MINOR[axis]
    major = size // minor
    offsets = [(a, b) for a in range(major) for b in range(minor) if a or b]
    return sorted(offsets, key=lambda o: -ring(major, o[0]) - ring(minor, o[1]) * (axis == "view"))


def neighbour(me, offset, axis, size):
    minor = MINOR[axis]
    major = size // minor

    def wrap(value, limit):
        return jnp.where(value >= limit, value - limit, value)

    return wrap(lax.div(me, minor) + offset[0], major) * minor + wrap(
        lax.rem(me, minor) + offset[1], minor
    )


def exchange(axis, me, size, source, landing, send_sem, recv_sem):
    peers = [neighbour(me, offset, axis, size) for offset in farthest_first(axis, size)]

    def copy(peer, slot):
        return pltpu.make_async_remote_copy(
            src_ref=source(peer),
            dst_ref=landing.at[slot],
            send_sem=send_sem.at[peer],
            recv_sem=recv_sem.at[slot],
            device_id={axis: peer},
            device_id_type=pl.DeviceIdType.MESH,
        )

    for peer in peers:
        copy(peer, me).start()

    def arrived(peer):
        copy(peer, peer).wait_recv()

    def sent():
        for peer in peers:
            copy(peer, me).wait_send()

    return peers[::-1], arrived, sent


def greet(axis, me, size, barrier):
    for offset in farthest_first(axis, size):
        pl.semaphore_signal(
            barrier,
            inc=1,
            device_id={axis: neighbour(me, offset, axis, size)},
            device_id_type=pl.DeviceIdType.MESH,
        )


def split_rows(block):
    parts, lasts = [], []
    front, last = block[0:8], block[8:9]
    for _ in range(3):
        parts.append(front.astype(BF16).astype(F32))
        lasts.append(last.astype(BF16).astype(F32))
        front, last = front - parts[-1], last - lasts[-1]
    filler = jnp.zeros((5, LANES), F32)
    return jnp.concatenate(parts + lasts + [filler], axis=0).astype(BF16)


def by_distance(axis, size, cuts):
    major = size // MINOR[axis]
    return [
        [a for a in range(major) if low < ring(major, a) <= high]
        for low, high in zip((-1, *cuts), (*cuts, major))
    ]


def pick(axis, me, size, cuts, arrived, landing, high, hot):
    minor = MINOR[axis]
    total = None
    for group in by_distance(axis, size, cuts):
        numbers = []
        for a in group:
            for b in range(minor):
                if a or b:
                    arrived(neighbour(me, (a, b), axis, size))
            first = lax.div(neighbour(me, (a, 0), axis, size), minor) * (minor // 2)
            numbers += [first + k for k in range(minor // 2)]
        table = [
            jnp.concatenate([split_rows(landing[2 * n]), split_rows(landing[2 * n + 1])], axis=1)
            for n in numbers
        ]
        found = dot(jnp.concatenate(table, axis=0), hot)
        for k, n in enumerate(numbers):
            part = jnp.where(high == n, found[32 * k : 32 * k + 32], 0.0)
            total = part if total is None else total + part
    return total[0:8] + total[8:16] + total[16:24], total[24:25] + total[25:26] + total[26:27]


def scatter_sides(index, groups):
    count = index.shape[1]
    high, low = lax.shift_right_logical(index, 8), lax.bitwise_and(index, 255)
    mask = lax.broadcasted_iota(jnp.int32, (groups, count), 0) == high
    hot = lax.broadcasted_iota(jnp.int32, (256, count), 0) == low
    return high, mask, jnp.where(hot, 1.0, 0.0).astype(BF16)


def scatter(rows, mask, hot):
    return scattered(scatter_parts(rows, mask, hot), mask.shape[0], len(rows))


def scatter_parts(rows, mask, hot):
    sides = []
    for r, row in enumerate(rows):
        for _ in range(parts_of(r)):
            high = row.astype(BF16).astype(F32)
            sides.append(jnp.where(mask, high, 0.0))
            row = row - high
    if len(sides) * mask.shape[0] % 16:
        sides.append(jnp.zeros_like(sides[0]))
    return dot_nt(jnp.concatenate(sides, axis=0).astype(BF16), hot)


def parts_of(row):
    return 3 if row in FINE_ROWS else 2


def scattered(out, groups, count):
    sums, at = [], 0
    for r in range(count):
        sums.append(sum(out[groups * k : groups * (k + 1)] for k in range(at, at + parts_of(r))))
        at += parts_of(r)
    return sums


def train_kernel(
    n_img,
    n_view,
    sizes,
    cameras_in,
    centers_in,
    scales_in,
    quats_in,
    logits_in,
    harm_in,
    slots_in,
    lists_in,
    counts_in,
    ids_in,
    grad_in,
    picture_ref,
    out_centers_ref,
    out_scales_ref,
    out_quats_ref,
    out_logits_ref,
    out_harm_ref,
    send_one,
    recv_one,
    send_two,
    recv_two,
    send_three,
    recv_three,
    send_four,
    recv_four,
    cameras_ref,
    centers_ref,
    scales_ref,
    quats_ref,
    logits_ref,
    harm_ref,
    slots_ref,
    lists_ref,
    counts_ref,
    ids_ref,
    grad_ref,
    slot_hot,
    entry_hot,
    view_sems,
    img_sems,
    load_sems,
):
    focal, half_w, half_h = sizes
    img, view = lax.axis_index("img"), lax.axis_index("view")
    barrier = pltpu.get_barrier_semaphore()
    loads = [
        pltpu.make_async_copy(source, target, load_sems.at[k])
        for k, (source, target) in enumerate(
            (
                (cameras_in, cameras_ref),
                (centers_in, centers_ref),
                (scales_in, scales_ref),
                (quats_in, quats_ref),
                (logits_in, logits_ref),
                (harm_in, harm_ref),
                (slots_in, slots_ref),
                (lists_in, lists_ref),
                (counts_in, counts_ref),
                (ids_in, ids_ref),
                (grad_in, grad_ref),
            )
        )
    ]
    for load in loads[:6]:
        load.start()
    greet("view", view, n_view, barrier)
    greet("img", img, n_img, barrier)
    for load in loads[6:]:
        load.start()
    for load in loads[:6]:
        load.wait()

    rot = rotations(cameras_ref[...], n_view)
    centers = [centers_ref[c : c + 1, :] for c in range(3)]
    unit, inv_norm, stretch, factor = shape_factor(
        [quats_ref[k : k + 1, :] for k in range(4)], [scales_ref[k : k + 1, :] for k in range(3)]
    )
    opacity = 1.0 / (1.0 + jnp.exp(-logits_ref[...]))
    values, saved = project(rot, centers, factor, harm_ref, focal, half_w, half_h)
    for r, value in enumerate(values):
        send_one[:, r, :] = value
    send_one[:, 8, :] = jnp.broadcast_to(opacity, (n_view, LANES))

    for load in loads[6:]:
        load.wait()
    pl.semaphore_wait(barrier, n_view + n_img - 2)
    peers, arrived, sent_one = exchange(
        "view", view, n_view, lambda p: send_one.at[p], recv_one, view_sems.at[0], view_sems.at[1]
    )

    slot_index = jnp.concatenate([slots_ref[d : d + 1, :] for d in range(n_img)], axis=1)
    slot_high, _, hot = scatter_sides(slot_index, n_view // 2)
    for d in range(n_img):
        slot_hot[d] = hot[:, LANES * d : LANES * d + LANES]
    recv_one[view] = send_one[view]
    geometry, last = pick("view", view, n_view, (1, 3), arrived, recv_one, slot_high, hot)
    for d in range(n_img):
        send_two[d, 0:8, :] = geometry[:, LANES * d : LANES * d + LANES]
        send_two[d, 8:9, :] = last[:, LANES * d : LANES * d + LANES]

    peers, arrived, sent_two = exchange(
        "img", img, n_img, lambda p: send_two.at[p], recv_two, img_sems.at[0], img_sems.at[1]
    )

    tiles = lists_ref.shape[0]
    lists = lists_ref[...]
    entry_index = jnp.concatenate([lists[t : t + 1] for t in range(tiles)], axis=1)
    entry_high, entry_mask, hot = scatter_sides(entry_index, n_img // 2)
    entry_hot[...] = hot
    before, after = triangle(False), triangle(True)
    pixels = []
    for t in range(tiles):
        grad = grad_ref[:, t, :]
        high = grad.astype(BF16).astype(F32)
        columns = jnp.concatenate([high, high, grad - high], axis=0).T.astype(BF16)
        pixels.append((split_two(grad), columns))
    recv_two[img] = send_two[img]
    geometry, last = pick("img", img, n_img, (3,), arrived, recv_two, entry_high, hot)
    work = []
    for t in range(tiles):
        at = slice(PIX * t, PIX * t + PIX)
        work.append(Tile(geometry[:, at], last[:, at], counts_ref[t], ids_ref[t], *pixels[t]))
    rendered = render(work, before, after)
    for t in range(tiles):
        picture_ref[:, t, :] = rendered[t][0]

    rows = [jnp.concatenate([grads[r] for _, grads in rendered], axis=1) for r in range(ROWS)]
    for r, total in enumerate(scatter(rows, entry_mask, entry_hot[...])):
        for h in range(2):
            send_three[:, h, r, :] = total[:, LANES * h : LANES * h + LANES]
    peers, arrived, sent_three = exchange(
        "img",
        img,
        n_img,
        lambda p: send_three.at[lax.div(p, 2), lax.rem(p, 2)],
        recv_three,
        img_sems.at[2],
        img_sems.at[3],
    )
    recv_three[img] = send_three[lax.div(img, 2), lax.rem(img, 2)]
    out = None
    for group in by_distance("img", n_img, (1, 3)):
        places = []
        for a in group:
            for b in range(MINOR["img"]):
                places.append(neighbour(img, (a, b), "img", n_img))
                if a or b:
                    arrived(places[-1])
        rows = [
            jnp.concatenate([recv_three[p, r : r + 1, :] for p in places], axis=1) for r in range(ROWS)
        ]
        high = lax.shift_right_logical(
            jnp.concatenate([slots_ref[pl.ds(p, 1), :] for p in places], axis=1), 8
        )
        mask = lax.broadcasted_iota(jnp.int32, (n_view // 2, high.shape[1]), 0) == high
        part = scatter_parts(rows, mask, jnp.concatenate([slot_hot[p] for p in places], axis=1))
        out = part if out is None else out + part
    for r, total in enumerate(scattered(out, n_view // 2, ROWS)):
        for h in range(2):
            send_four[:, h, r, :] = total[:, LANES * h : LANES * h + LANES]
    peers, arrived, sent_four = exchange(
        "view",
        view,
        n_view,
        lambda p: send_four.at[lax.div(p, 2), lax.rem(p, 2)],
        recv_four,
        view_sems.at[2],
        view_sems.at[3],
    )
    recv_four[view] = send_four[lax.div(view, 2), lax.rem(view, 2)]
    sent_one()
    sent_two()
    sent_three()
    sent_four()

    for peer in peers:
        arrived(peer)

    grads = [recv_four[:, r, :] for r in range(ROWS)]
    dcenters, dfactor = project_back(rot, factor, harm_ref, focal, saved, grads, out_harm_ref)
    dscale, dquat = shape_back(unit, inv_norm, stretch, factor, dfactor)
    for c in range(3):
        out_centers_ref[c : c + 1, :] = dcenters[c]
        out_scales_ref[c : c + 1, :] = dscale[c]
    for k in range(4):
        out_quats_ref[k : k + 1, :] = dquat[k]
    out_logits_ref[...] = over_cameras(grads[8]) * opacity * (1.0 - opacity)


def place_kernel(*refs):
    *arrays, sems = refs
    count = len(arrays) // 2
    moves = [
        pltpu.make_async_copy(arrays[k], arrays[count + k], sems.at[k]) for k in range(count)
    ]
    for move in moves:
        move.start()
    for move in moves:
        move.wait()


def per_device(
    centers,
    log_scales,
    quaternions,
    logits,
    harmonics,
    cameras,
    tile_lists,
    tile_counts,
    tile_ids,
    send_index,
    pixel_grad,
):
    n_img, n_view = lax.axis_size("img"), lax.axis_size("view")
    tiles = tile_ids.shape[2]
    sizes = (16.0 * TW, 8.0 * TW, 8.0 * (n_img * tiles // TW))
    vmem, hbm = pl.BlockSpec(memory_space=pltpu.VMEM), pl.BlockSpec(memory_space=pltpu.HBM)
    per_view, per_img = (n_view, ROWS, LANES), (n_img, ROWS, LANES)
    inputs = (
        cameras.T,
        centers,
        log_scales,
        quaternions,
        logits.reshape(1, -1),
        harmonics,
        send_index[0, 0],
        tile_lists[0, 0],
        tile_counts[0, 0],
        tile_ids[0, 0],
        pixel_grad[0, 0].transpose(1, 0, 2),
    )
    shapes = [
        jax.ShapeDtypeStruct((3, tiles, PIX), F32),
        jax.ShapeDtypeStruct((3, LANES), F32),
        jax.ShapeDtypeStruct((3, LANES), F32),
        jax.ShapeDtypeStruct((4, LANES), F32),
        jax.ShapeDtypeStruct((1, LANES), F32),
        jax.ShapeDtypeStruct((48, LANES), F32),
    ]
    results = pl.pallas_call(
        functools.partial(train_kernel, n_img, n_view, sizes),
        out_shape=[pltpu.VMEM(shape.shape, shape.dtype) for shape in shapes],
        in_specs=[hbm] * len(inputs),
        out_specs=[vmem] * len(shapes),
        scratch_shapes=[
            pltpu.VMEM(per_view, F32),
            pltpu.VMEM(per_view, F32),
            pltpu.VMEM(per_img, F32),
            pltpu.VMEM(per_img, F32),
            pltpu.VMEM((n_img // 2, 2, ROWS, LANES), F32),
            pltpu.VMEM(per_img, F32),
            pltpu.VMEM((n_view // 2, 2, ROWS, LANES), F32),
            pltpu.VMEM(per_view, F32),
        ]
        + [
            (pltpu.SMEM if value.shape == (tiles,) else pltpu.VMEM)(value.shape, value.dtype)
            for value in inputs
        ]
        + [
            pltpu.VMEM((n_img, 256, LANES), BF16),
            pltpu.VMEM((256, tiles * PIX), BF16),
            pltpu.SemaphoreType.DMA((4, n_view)),
            pltpu.SemaphoreType.DMA((4, n_img)),
            pltpu.SemaphoreType.DMA((len(inputs),)),
        ],
        compiler_params=pltpu.CompilerParams(
            collective_id=0, has_side_effects=True, vmem_limit_bytes=63 * 1024 * 1024
        ),
    )(*inputs)
    out = pl.pallas_call(
        place_kernel,
        out_shape=shapes,
        in_specs=[vmem] * len(shapes),
        out_specs=[hbm] * len(shapes),
        scratch_shapes=[pltpu.SemaphoreType.DMA((len(shapes),))],
    )(*(pltpu.with_memory_space_constraint(value, pltpu.VMEM) for value in results))
    picture = out[0].transpose(1, 0, 2)[None, None]
    return (picture, out[1], out[2], out[3], out[4].reshape(-1), out[5])


def solution(mesh):
    split = P(None, ("img", "view"))
    placed = (
        split,
        split,
        split,
        P(("img", "view")),
        split,
        P(),
        P("view", "img", None, None),
        P("view", "img", None),
        P("view", "img", None),
        P("view", "img", None, None),
        P("view", "img", None, None, None),
    )
    return jax.shard_map(
        per_device,
        mesh=mesh,
        in_specs=placed,
        out_specs=(P("view", "img", None, None, None), split, split, split, P(("img", "view")), split),
        check_vma=False,
    )
```

```python
import functools

import jax
import jax.numpy as jnp
from jax import lax
from jax.experimental import pallas as pl
from jax.experimental.pallas import tpu as pltpu
from jax.sharding import PartitionSpec as P

TW = 8
ROWS = 9
LANES = 128
PIX = 256
MINOR = {"view": 4, "img": 2}
LINES = 16
FINE_ROWS = (2, 3, 4)
LOG2E = 1.4426950408889634
CAMERA_DISTANCE = 4.0
C0 = 0.28209479177387814
C1 = 0.4886025119029199
C20, C21, C22, C23, C24 = (
    1.0925484305920792,
    -1.0925484305920792,
    0.31539156525252005,
    -1.0925484305920792,
    0.5462742152960396,
)
C30, C31, C32, C33, C34, C35, C36 = (
    -0.5900435899266435,
    2.890611442640554,
    -0.4570457994644658,
    0.3731763325901154,
    -0.4570457994644658,
    1.445305721320277,
    -0.5900435899266435,
)
F32 = jnp.float32
BF16 = jnp.bfloat16


def split_two(value):
    high = value.astype(BF16)
    low = (value - high.astype(F32)).astype(BF16)
    return high, low


def dot(left, right):
    return lax.dot_general(left, right, (((1,), (0,)), ((), ())), preferred_element_type=F32)


def dot_nt(left, right):
    return lax.dot_general(left, right, (((1,), (1,)), ((), ())), preferred_element_type=F32)


def rotations(cameras, count):
    turns = jnp.concatenate([jnp.cos(cameras), jnp.sin(cameras)], axis=0).T
    ca, cb, cg, sa, sb, sg = (
        jnp.broadcast_to(turns[:, k : k + 1], (count, LANES)) for k in range(6)
    )
    return [
        [cg * ca, cg * sa * sb - sg * cb, cg * sa * cb + sg * sb],
        [sg * ca, sg * sa * sb + cg * cb, sg * sa * cb - cg * sb],
        [-sa, ca * sb, ca * cb],
    ]


def shape_factor(quats, scales):
    inv = lax.rsqrt(sum(q * q for q in quats))
    w, x, y, z = (q * inv for q in quats)
    rot = [
        [1.0 - 2.0 * (y * y + z * z), 2.0 * (x * y - w * z), 2.0 * (x * z + w * y)],
        [2.0 * (x * y + w * z), 1.0 - 2.0 * (x * x + z * z), 2.0 * (y * z - w * x)],
        [2.0 * (x * z - w * y), 2.0 * (y * z + w * x), 1.0 - 2.0 * (x * x + y * y)],
    ]
    stretch = [jnp.exp(s) for s in scales]
    factor = [[rot[r][k] * stretch[k] for k in range(3)] for r in range(3)]
    return (w, x, y, z), inv, stretch, factor


def basis_of(x, y, z):
    xx, yy, zz = x * x, y * y, z * z
    return [
        None,
        -C1 * y,
        C1 * z,
        -C1 * x,
        C20 * x * y,
        C21 * y * z,
        C22 * (2.0 * zz - xx - yy),
        C23 * x * z,
        C24 * (xx - yy),
        C30 * y * (3.0 * xx - yy),
        C31 * x * y * z,
        C32 * y * (4.0 * zz - xx - yy),
        C33 * z * (2.0 * zz - 3.0 * xx - 3.0 * yy),
        C34 * x * (4.0 * zz - xx - yy),
        C35 * z * (xx - yy),
        C36 * x * (xx - 3.0 * yy),
    ]


def project(rot, centers, factor, harm_ref, focal, half_w, half_h):
    pts = [rot[r][0] * centers[0] + rot[r][1] * centers[1] + rot[r][2] * centers[2] for r in range(3)]
    iz = 1.0 / (pts[2] + CAMERA_DISTANCE)
    fiz = focal * iz
    tx, ty = pts[0] * iz, pts[1] * iz
    t0 = [fiz * (rot[0][c] - tx * rot[2][c]) for c in range(3)]
    t1 = [fiz * (rot[1][c] - ty * rot[2][c]) for c in range(3)]
    s0 = [t0[0] * factor[0][k] + t0[1] * factor[1][k] + t0[2] * factor[2][k] for k in range(3)]
    s1 = [t1[0] * factor[0][k] + t1[1] * factor[1][k] + t1[2] * factor[2][k] for k in range(3)]
    cov_a = s0[0] * s0[0] + s0[1] * s0[1] + s0[2] * s0[2] + 0.3
    cov_b = s0[0] * s1[0] + s0[1] * s1[1] + s0[2] * s1[2]
    cov_c = s1[0] * s1[0] + s1[1] * s1[1] + s1[2] * s1[2] + 0.3
    inv_det = 1.0 / (cov_a * cov_c - cov_b * cov_b)
    conic = (cov_c * inv_det, -cov_b * inv_det, cov_a * inv_det)
    offs = [centers[c] + CAMERA_DISTANCE * rot[2][c] for c in range(3)]
    inv_len = lax.rsqrt(offs[0] * offs[0] + offs[1] * offs[1] + offs[2] * offs[2])
    x, y, z = (o * inv_len for o in offs)
    basis = basis_of(x, y, z)
    shade = []
    for ch in range(3):
        total = 0.5 + C0 * harm_ref[ch : ch + 1, :]
        for l in range(1, 16):
            total = total + basis[l] * harm_ref[3 * l + ch : 3 * l + ch + 1, :]
        shade.append(total)
    colour = [jnp.maximum(s, 0.0) for s in shade]
    values = [focal * tx + half_w, focal * ty + half_h, *conic, *colour]
    saved = (iz, fiz, tx, ty, t0, t1, s0, s1, conic, inv_det, inv_len, (x, y, z), basis, shade)
    return values, saved


def over_cameras(value):
    return jnp.sum(value, axis=0, keepdims=True)


def project_back(rot, factor, harm_ref, focal, saved, grads, grad_harm_ref):
    iz, fiz, tx, ty, t0, t1, s0, s1, conic, inv_det, inv_len, (x, y, z), basis, shade = saved
    du, dv, dca, dcb, dcc = grads[:5]
    dcol = []
    for ch in range(3):
        g = grads[5 + ch]
        dcol.append(jnp.where(shade[ch] > 0.0, g, jnp.where(shade[ch] == 0.0, 0.5 * g, 0.0)))
    e = [None]
    for ch in range(3):
        grad_harm_ref[ch : ch + 1, :] = C0 * over_cameras(dcol[ch])
    for l in range(1, 16):
        e.append(sum(harm_ref[3 * l + ch : 3 * l + ch + 1, :] * dcol[ch] for ch in range(3)))
        for ch in range(3):
            grad_harm_ref[3 * l + ch : 3 * l + ch + 1, :] = over_cameras(basis[l] * dcol[ch])
    xx, yy, zz, xy, yz, xz = x * x, y * y, z * z, x * y, y * z, x * z
    dx = (
        -C1 * e[3]
        + C20 * y * e[4]
        + x * (2.0 * C24 * e[8] - 2.0 * C22 * e[6])
        + C23 * z * e[7]
        + xy * (6.0 * C30 * e[9] - 2.0 * C32 * e[11])
        + C31 * yz * e[10]
        + xz * (2.0 * C35 * e[14] - 6.0 * C33 * e[12])
        + C34 * (4.0 * zz - 3.0 * xx - yy) * e[13]
        + 3.0 * C36 * (xx - yy) * e[15]
    )
    dy = (
        -C1 * e[1]
        + C20 * x * e[4]
        + C21 * z * e[5]
        - y * (2.0 * C22 * e[6] + 2.0 * C24 * e[8])
        + 3.0 * C30 * (xx - yy) * e[9]
        + C31 * xz * e[10]
        + C32 * (4.0 * zz - xx - 3.0 * yy) * e[11]
        - yz * (6.0 * C33 * e[12] + 2.0 * C35 * e[14])
        - xy * (2.0 * C34 * e[13] + 6.0 * C36 * e[15])
    )
    dz = (
        C1 * e[2]
        + C21 * y * e[5]
        + 4.0 * C22 * z * e[6]
        + C23 * x * e[7]
        + C31 * xy * e[10]
        + 8.0 * C32 * yz * e[11]
        + C33 * (6.0 * zz - 3.0 * xx - 3.0 * yy) * e[12]
        + 8.0 * C34 * xz * e[13]
        + C35 * (xx - yy) * e[14]
    )
    along = x * dx + y * dy + z * dz
    doff = [inv_len * (dx - x * along), inv_len * (dy - y * along), inv_len * (dz - z * along)]
    ca, cb, cc = conic
    s = dca * ca + dcb * cb + dcc * cc
    da = inv_det * dcc - s * ca
    dc = inv_det * dca - s * cc
    db = -(inv_det * dcb) - 2.0 * s * cb
    da2, dc2 = da + da, dc + dc
    ds0 = [da2 * s0[k] + db * s1[k] for k in range(3)]
    ds1 = [dc2 * s1[k] + db * s0[k] for k in range(3)]
    dt0 = [sum(ds0[k] * factor[c][k] for k in range(3)) for c in range(3)]
    dt1 = [sum(ds1[k] * factor[c][k] for k in range(3)) for c in range(3)]
    dfactor = [[over_cameras(t0[c] * ds0[k] + t1[c] * ds1[k]) for k in range(3)] for c in range(3)]
    n0 = sum(dt0[c] * rot[2][c] for c in range(3))
    n1 = sum(dt1[c] * rot[2][c] for c in range(3))
    m0 = sum(dt0[c] * rot[0][c] for c in range(3))
    m1 = sum(dt1[c] * rot[1][c] for c in range(3))
    dfiz = (m0 - tx * n0) + (m1 - ty * n1)
    dtx = focal * du - fiz * n0
    dty = focal * dv - fiz * n1
    dp = [dtx * iz, dty * iz, -iz * (fiz * dfiz + dtx * tx + dty * ty)]
    dcenters = [
        over_cameras(sum(rot[r][c] * dp[r] for r in range(3)) + doff[c]) for c in range(3)
    ]
    return dcenters, dfactor


def shape_back(unit, inv, stretch, factor, dfactor):
    w, x, y, z = unit
    dscale = [sum(factor[r][k] * dfactor[r][k] for r in range(3)) for k in range(3)]
    d = [[dfactor[r][k] * stretch[k] for k in range(3)] for r in range(3)]
    dw = 2.0 * (z * (d[1][0] - d[0][1]) + y * (d[0][2] - d[2][0]) + x * (d[2][1] - d[1][2]))
    dx = 2.0 * (
        y * (d[0][1] + d[1][0]) + z * (d[0][2] + d[2][0]) + w * (d[2][1] - d[1][2])
    ) - 4.0 * x * (d[1][1] + d[2][2])
    dy = 2.0 * (
        x * (d[0][1] + d[1][0]) + z * (d[1][2] + d[2][1]) + w * (d[0][2] - d[2][0])
    ) - 4.0 * y * (d[0][0] + d[2][2])
    dz = 2.0 * (
        x * (d[0][2] + d[2][0]) + y * (d[1][2] + d[2][1]) + w * (d[1][0] - d[0][1])
    ) - 4.0 * z * (d[0][0] + d[1][1])
    along = w * dw + x * dx + y * dy + z * dz
    dquat = [inv * (g - q * along) for g, q in zip((dw, dx, dy, dz), unit)]
    return dscale, dquat


def lane_pick(table, lanes):
    return jnp.take_along_axis(table, lanes, axis=1, mode="promise_in_bounds")


def triangle(later):
    row = lax.broadcasted_iota(jnp.int32, (PIX, PIX), 0)
    col = lax.broadcasted_iota(jnp.int32, (PIX, PIX), 1)
    return jnp.where(row > col if later else row < col, 1.0, 0.0).astype(BF16)


class Tile:
    def __init__(self, geometry, opacity, count, number, grad, grad_t):
        entry = lax.broadcasted_iota(jnp.int32, (1, PIX), 1)
        self.live = jnp.where(entry < count, opacity, 0.0)
        self.opacity = opacity
        left = (16 * lax.rem(number, TW) + 8).astype(F32)
        top = (16 * lax.div(number, TW) + 8).astype(F32)
        self.u, self.v = geometry[0:1] - left, geometry[1:2] - top
        self.conic = geometry[2:3], geometry[3:4], geometry[4:5]
        ca, cb, cc = self.conic
        self.local = lax.broadcasted_iota(jnp.int32, (16, PIX), 0).astype(F32) - 7.5
        dx, self.dy = self.local - self.u, self.local - self.v
        self.part_a = (-0.5 * LOG2E * ca) * dx * dx
        self.part_b = (-LOG2E * cb) * dx
        self.part_c = (-0.5 * LOG2E * cc) * self.dy * self.dy
        self.colour = split_two(geometry[5:8])
        self.grad, self.grad_t = grad, grad_t
        c_hi, c_lo = self.colour
        self.mix = jnp.concatenate([c_hi, c_lo, c_hi], axis=0)
        self.moments = [None, None, None]
        self.weights = []

    def shade(self, at, before):
        alphas = []
        for line in range(at, at + LINES):
            power = self.part_a + self.part_b * self.dy[line : line + 1] + self.part_c[line : line + 1]
            alphas.append(self.live * jnp.exp2(power))
        alpha = jnp.concatenate(alphas, axis=0)
        log_left = jnp.log2(1.0 - alpha)
        log_hi, log_lo = split_two(log_left)
        reach = dot(self.grad_t[16 * at : 16 * (at + LINES)], self.mix)
        return at, alpha, log_left, dot(log_hi, before) + dot(log_lo, before), reach

    def weigh(self, shaded, after):
        at, alpha, log_left, log_trans, reach = shaded
        weight = alpha * jnp.exp2(log_trans)
        gain = weight * reach
        g_hi, g_lo = split_two(gain)
        self.weights.append(split_two(weight))
        return at, alpha, log_left, gain, dot(g_hi, after) + dot(g_lo, after)

    def collect(self, weighed):
        at, alpha, log_left, gain, behind = weighed
        back = gain - behind * (alpha * jnp.exp2(-log_left))
        for k in range(LINES):
            piece = back[16 * k : 16 * k + 16]
            level = at + k - 7.5
            terms = (piece, level * piece, (level * level) * piece)
            for m in range(3):
                self.moments[m] = terms[m] if self.moments[m] is None else self.moments[m] + terms[m]

    def picture(self):
        c_hi, c_lo = self.colour
        w_hi, w_lo = self.weights
        first = dot_nt(jnp.concatenate([c_hi, c_lo], axis=0), w_hi)
        return first[0:3] + first[3:6] + dot_nt(c_hi, w_lo)

    def finish(self):
        w_hi = jnp.concatenate([w[0] for w in self.weights], axis=0)
        w_lo = jnp.concatenate([w[1] for w in self.weights], axis=0)
        self.weights = w_hi, w_lo
        g_hi, g_lo = self.grad
        first = dot(jnp.concatenate([g_hi, g_lo], axis=0), w_hi)
        dcolour = first[0:3] + first[3:6] + dot(g_hi, w_lo)

        def total(value):
            return jnp.sum(value, axis=0, keepdims=True)

        u, v, (ca, cb, cc), local = self.u, self.v, self.conic, self.local
        m0, my, myy = (total(m) for m in self.moments)
        mx, mxy = total(local * self.moments[0]), total(local * self.moments[1])
        mxx = total(local * local * self.moments[0])
        qx, qy = mx - u * m0, my - v * m0
        qxx = mxx - u * (mx + qx)
        qyy = myy - v * (my + qy)
        qxy = mxy - u * my - v * qx
        grads = [
            ca * qx + cb * qy,
            cb * qx + cc * qy,
            -0.5 * qxx,
            -qxy,
            -0.5 * qyy,
            dcolour[0:1],
            dcolour[1:2],
            dcolour[2:3],
            m0 / self.opacity,
        ]
        return grads


def render(tiles, before, after):
    parts = [(tile, at) for tile in tiles for at in range(0, 16, LINES)]
    shaded, weighed, done = [], [], []
    for step in range(len(parts) + 2):
        if step >= 2:
            tile, at = parts[step - 2]
            tile.collect(weighed[step - 2])
            weighed[step - 2] = None
            if at + LINES == 16:
                done.append(tile.finish())
        if 1 <= step <= len(parts):
            weighed.append(parts[step - 1][0].weigh(shaded[step - 1], after))
            shaded[step - 1] = None
        if step < len(parts):
            shaded.append(parts[step][0].shade(parts[step][1], before))
    return done


def ring(size, steps):
    return min(steps, size - steps)


def farthest_first(axis, size):
    minor = MINOR[axis]
    major = size // minor
    offsets = [(a, b) for a in range(major) for b in range(minor) if a or b]
    return sorted(offsets, key=lambda o: -ring(major, o[0]) - ring(minor, o[1]) * (axis == "view"))


def neighbour(me, offset, axis, size):
    minor = MINOR[axis]
    major = size // minor

    def wrap(value, limit):
        return jnp.where(value >= limit, value - limit, value)

    return wrap(lax.div(me, minor) + offset[0], major) * minor + wrap(
        lax.rem(me, minor) + offset[1], minor
    )


def exchange(axis, me, size, source, landing, send_sem, recv_sem):
    def peers(places=None):
        return [
            neighbour(me, offset, axis, size)
            for offset in farthest_first(axis, size)
            if places is None or offset[0] in places
        ]

    def copy(peer, slot):
        return pltpu.make_async_remote_copy(
            src_ref=source(peer),
            dst_ref=landing.at[slot],
            send_sem=send_sem.at[peer],
            recv_sem=recv_sem.at[slot],
            device_id={axis: peer},
            device_id_type=pl.DeviceIdType.MESH,
        )

    def start(places=None):
        for peer in peers(places):
            copy(peer, me).start()

    def arrived(peer):
        copy(peer, peer).wait_recv()

    def sent():
        for peer in peers():
            copy(peer, me).wait_send()

    return start, arrived, sent


def greet(axis, me, size, barrier):
    for offset in farthest_first(axis, size):
        pl.semaphore_signal(
            barrier,
            inc=1,
            device_id={axis: neighbour(me, offset, axis, size)},
            device_id_type=pl.DeviceIdType.MESH,
        )


def split_rows(block):
    parts, lasts = [], []
    front, last = block[0:8], block[8:9]
    for _ in range(3):
        parts.append(front.astype(BF16).astype(F32))
        lasts.append(last.astype(BF16).astype(F32))
        front, last = front - parts[-1], last - lasts[-1]
    filler = jnp.zeros((5, LANES), F32)
    return jnp.concatenate(parts + lasts + [filler], axis=0).astype(BF16)


def by_distance(axis, size, cuts):
    major = size // MINOR[axis]
    return [
        [a for a in range(major) if low < ring(major, a) <= high]
        for low, high in zip((-1, *cuts), (*cuts, major))
    ]


def pick(axis, me, size, cuts, arrived, landing, high, hot):
    minor = MINOR[axis]
    total = None
    for group in by_distance(axis, size, cuts):
        numbers = []
        for a in group:
            for b in range(minor):
                if a or b:
                    arrived(neighbour(me, (a, b), axis, size))
            first = lax.div(neighbour(me, (a, 0), axis, size), minor) * (minor // 2)
            numbers += [first + k for k in range(minor // 2)]
        table = [
            jnp.concatenate([split_rows(landing[2 * n]), split_rows(landing[2 * n + 1])], axis=1)
            for n in numbers
        ]
        found = dot(jnp.concatenate(table, axis=0), hot)
        for k, n in enumerate(numbers):
            part = jnp.where(high == n, found[32 * k : 32 * k + 32], 0.0)
            total = part if total is None else total + part
    return total[0:8] + total[8:16] + total[16:24], total[24:25] + total[25:26] + total[26:27]


def scatter_sides(index, groups):
    count = index.shape[1]
    high, low = lax.shift_right_logical(index, 8), lax.bitwise_and(index, 255)
    mask = lax.broadcasted_iota(jnp.int32, (groups, count), 0) == high
    hot = lax.broadcasted_iota(jnp.int32, (256, count), 0) == low
    return high, mask, jnp.where(hot, 1.0, 0.0).astype(BF16)


def scatter(rows, mask, hot):
    return scattered(scatter_parts(rows, mask, hot), mask.shape[0], len(rows))


def scatter_parts(rows, mask, hot):
    sides = []
    for r, row in enumerate(rows):
        for _ in range(parts_of(r)):
            high = row.astype(BF16).astype(F32)
            sides.append(jnp.where(mask, high, 0.0))
            row = row - high
    if len(sides) * mask.shape[0] % 16:
        sides.append(jnp.zeros_like(sides[0]))
    return dot_nt(jnp.concatenate(sides, axis=0).astype(BF16), hot)


def parts_of(row):
    return 3 if row in FINE_ROWS else 2


def scattered(out, groups, count):
    sums, at = [], 0
    for r in range(count):
        sums.append(sum(out[groups * k : groups * (k + 1)] for k in range(at, at + parts_of(r))))
        at += parts_of(r)
    return sums


def train_kernel(
    n_img,
    n_view,
    sizes,
    cameras_in,
    centers_in,
    scales_in,
    quats_in,
    logits_in,
    harm_in,
    slots_in,
    lists_in,
    counts_in,
    ids_in,
    grad_in,
    picture_ref,
    out_centers_ref,
    out_scales_ref,
    out_quats_ref,
    out_logits_ref,
    out_harm_ref,
    send_one,
    recv_one,
    send_two,
    recv_two,
    send_three,
    recv_three,
    send_four,
    recv_four,
    cameras_ref,
    centers_ref,
    scales_ref,
    quats_ref,
    logits_ref,
    harm_ref,
    slots_ref,
    lists_ref,
    counts_ref,
    ids_ref,
    grad_ref,
    slot_hot,
    entry_hot,
    view_sems,
    img_sems,
    load_sems,
):
    focal, half_w, half_h = sizes
    img, view = lax.axis_index("img"), lax.axis_index("view")
    barrier = pltpu.get_barrier_semaphore()
    loads = [
        pltpu.make_async_copy(source, target, load_sems.at[k])
        for k, (source, target) in enumerate(
            (
                (cameras_in, cameras_ref),
                (centers_in, centers_ref),
                (scales_in, scales_ref),
                (quats_in, quats_ref),
                (logits_in, logits_ref),
                (harm_in, harm_ref),
                (slots_in, slots_ref),
                (lists_in, lists_ref),
                (counts_in, counts_ref),
                (ids_in, ids_ref),
                (grad_in, grad_ref),
            )
        )
    ]
    for load in loads[:6]:
        load.start()
    greet("view", view, n_view, barrier)
    greet("img", img, n_img, barrier)
    for load in loads[6:]:
        load.start()
    for load in loads[:6]:
        load.wait()

    rot = rotations(cameras_ref[...], n_view)
    centers = [centers_ref[c : c + 1, :] for c in range(3)]
    unit, inv_norm, stretch, factor = shape_factor(
        [quats_ref[k : k + 1, :] for k in range(4)], [scales_ref[k : k + 1, :] for k in range(3)]
    )
    opacity = 1.0 / (1.0 + jnp.exp(-logits_ref[...]))
    values, saved = project(rot, centers, factor, harm_ref, focal, half_w, half_h)
    for r, value in enumerate(values):
        send_one[:, r, :] = value
    send_one[:, 8, :] = jnp.broadcast_to(opacity, (n_view, LANES))

    for load in loads[6:]:
        load.wait()
    pl.semaphore_wait(barrier, n_view + n_img - 2)
    start, arrived, sent_one = exchange(
        "view", view, n_view, lambda p: send_one.at[p], recv_one, view_sems.at[0], view_sems.at[1]
    )
    start()

    slot_index = jnp.concatenate([slots_ref[d : d + 1, :] for d in range(n_img)], axis=1)
    slot_high, _, hot = scatter_sides(slot_index, n_view // 2)
    for d in range(n_img):
        slot_hot[d] = hot[:, LANES * d : LANES * d + LANES]
    recv_one[view] = send_one[view]
    geometry, last = pick("view", view, n_view, (1, 3), arrived, recv_one, slot_high, hot)
    for d in range(n_img):
        send_two[d, 0:8, :] = geometry[:, LANES * d : LANES * d + LANES]
        send_two[d, 8:9, :] = last[:, LANES * d : LANES * d + LANES]

    start, arrived, sent_two = exchange(
        "img", img, n_img, lambda p: send_two.at[p], recv_two, img_sems.at[0], img_sems.at[1]
    )
    start()

    tiles = lists_ref.shape[0]
    lists = lists_ref[...]
    entry_index = jnp.concatenate([lists[t : t + 1] for t in range(tiles)], axis=1)
    entry_high, entry_mask, hot = scatter_sides(entry_index, n_img // 2)
    entry_hot[...] = hot
    before, after = triangle(False), triangle(True)
    pixels = []
    for t in range(tiles):
        grad = grad_ref[:, t, :]
        high = grad.astype(BF16).astype(F32)
        columns = jnp.concatenate([high, high, grad - high], axis=0).T.astype(BF16)
        pixels.append((split_two(grad), columns))
    recv_two[img] = send_two[img]
    geometry, last = pick("img", img, n_img, (3,), arrived, recv_two, entry_high, hot)
    work = []
    for t in range(tiles):
        at = slice(PIX * t, PIX * t + PIX)
        work.append(Tile(geometry[:, at], last[:, at], counts_ref[t], ids_ref[t], *pixels[t]))
    rendered = render(work, before, after)
    rows = [jnp.concatenate([grads[r] for grads in rendered], axis=1) for r in range(ROWS)]
    for r, total in enumerate(scatter(rows, entry_mask, entry_hot[...])):
        for h in range(2):
            send_three[:, h, r, :] = total[:, LANES * h : LANES * h + LANES]
    start, arrived, sent_three = exchange(
        "img",
        img,
        n_img,
        lambda p: send_three.at[lax.div(p, 2), lax.rem(p, 2)],
        recv_three,
        img_sems.at[2],
        img_sems.at[3],
    )
    start()
    recv_three[img] = send_three[lax.div(img, 2), lax.rem(img, 2)]
    for t in range(tiles):
        picture_ref[:, t, :] = work[t].picture()
    start, arrived_home, sent_four = exchange(
        "view",
        view,
        n_view,
        lambda p: send_four.at[lax.div(p, 2), lax.rem(p, 2)],
        recv_four,
        view_sems.at[2],
        view_sems.at[3],
    )
    minor = MINOR["view"]
    major, pairs = n_view // minor, minor // 2
    places = sorted(range(major), key=lambda a: -ring(major, a))
    numbers = []
    for a in places:
        first = lax.div(neighbour(view, (a, 0), "view", n_view), minor) * pairs
        numbers += [first + k for k in range(pairs)]
    row = lax.broadcasted_iota(jnp.int32, (len(numbers), 1), 0)
    order = sum(jnp.where(row == k, n, 0) for k, n in enumerate(numbers))
    half = len(numbers) // 2
    sums = []
    groups = by_distance("img", n_img, (1, 3))
    for group in groups:
        blocks = []
        for a in group:
            for b in range(MINOR["img"]):
                blocks.append(neighbour(img, (a, b), "img", n_img))
                if a or b:
                    arrived(blocks[-1])
        rows = [
            jnp.concatenate([recv_three[p, r : r + 1, :] for p in blocks], axis=1) for r in range(ROWS)
        ]
        high = lax.shift_right_logical(
            jnp.concatenate([slots_ref[pl.ds(p, 1), :] for p in blocks], axis=1), 8
        )
        hot = jnp.concatenate([slot_hot[p] for p in blocks], axis=1)
        for h in range(2):
            mask = order[half * h : half * h + half] == high
            part = scatter_parts(rows, mask, hot)
            if group is groups[0]:
                sums.append(part)
            else:
                sums[h] = sums[h] + part
            if group is groups[-1]:
                for r, total in enumerate(scattered(sums[h], half, ROWS)):
                    for k in range(half):
                        for side in range(2):
                            send_four[numbers[half * h + k], side, r : r + 1, :] = total[
                                k : k + 1, LANES * side : LANES * side + LANES
                            ]
                start(places[major // 2 * h : major // 2 * (h + 1)])
    recv_four[view] = send_four[lax.div(view, 2), lax.rem(view, 2)]
    sent_one()
    sent_two()
    sent_three()
    sent_four()

    for offset in farthest_first("view", n_view)[::-1]:
        arrived_home(neighbour(view, offset, "view", n_view))

    grads = [recv_four[:, r, :] for r in range(ROWS)]
    dcenters, dfactor = project_back(rot, factor, harm_ref, focal, saved, grads, out_harm_ref)
    dscale, dquat = shape_back(unit, inv_norm, stretch, factor, dfactor)
    for c in range(3):
        out_centers_ref[c : c + 1, :] = dcenters[c]
        out_scales_ref[c : c + 1, :] = dscale[c]
    for k in range(4):
        out_quats_ref[k : k + 1, :] = dquat[k]
    out_logits_ref[...] = over_cameras(grads[8]) * opacity * (1.0 - opacity)


def place_kernel(*refs):
    *arrays, sems = refs
    count = len(arrays) // 2
    moves = [
        pltpu.make_async_copy(arrays[k], arrays[count + k], sems.at[k]) for k in range(count)
    ]
    for move in moves:
        move.start()
    for move in moves:
        move.wait()


def per_device(
    centers,
    log_scales,
    quaternions,
    logits,
    harmonics,
    cameras,
    tile_lists,
    tile_counts,
    tile_ids,
    send_index,
    pixel_grad,
):
    n_img, n_view = lax.axis_size("img"), lax.axis_size("view")
    tiles = tile_ids.shape[2]
    sizes = (16.0 * TW, 8.0 * TW, 8.0 * (n_img * tiles // TW))
    vmem, hbm = pl.BlockSpec(memory_space=pltpu.VMEM), pl.BlockSpec(memory_space=pltpu.HBM)
    per_view, per_img = (n_view, ROWS, LANES), (n_img, ROWS, LANES)
    inputs = (
        cameras.T,
        centers,
        log_scales,
        quaternions,
        logits.reshape(1, -1),
        harmonics,
        send_index[0, 0],
        tile_lists[0, 0],
        tile_counts[0, 0],
        tile_ids[0, 0],
        pixel_grad[0, 0].transpose(1, 0, 2),
    )
    shapes = [
        jax.ShapeDtypeStruct((3, tiles, PIX), F32),
        jax.ShapeDtypeStruct((3, LANES), F32),
        jax.ShapeDtypeStruct((3, LANES), F32),
        jax.ShapeDtypeStruct((4, LANES), F32),
        jax.ShapeDtypeStruct((1, LANES), F32),
        jax.ShapeDtypeStruct((48, LANES), F32),
    ]
    results = pl.pallas_call(
        functools.partial(train_kernel, n_img, n_view, sizes),
        out_shape=[pltpu.VMEM(shape.shape, shape.dtype) for shape in shapes],
        in_specs=[hbm] * len(inputs),
        out_specs=[vmem] * len(shapes),
        scratch_shapes=[
            pltpu.VMEM(per_view, F32),
            pltpu.VMEM(per_view, F32),
            pltpu.VMEM(per_img, F32),
            pltpu.VMEM(per_img, F32),
            pltpu.VMEM((n_img // 2, 2, ROWS, LANES), F32),
            pltpu.VMEM(per_img, F32),
            pltpu.VMEM((n_view // 2, 2, ROWS, LANES), F32),
            pltpu.VMEM(per_view, F32),
        ]
        + [
            (pltpu.SMEM if value.shape == (tiles,) else pltpu.VMEM)(value.shape, value.dtype)
            for value in inputs
        ]
        + [
            pltpu.VMEM((n_img, 256, LANES), BF16),
            pltpu.VMEM((256, tiles * PIX), BF16),
            pltpu.SemaphoreType.DMA((4, n_view)),
            pltpu.SemaphoreType.DMA((4, n_img)),
            pltpu.SemaphoreType.DMA((len(inputs),)),
        ],
        compiler_params=pltpu.CompilerParams(
            collective_id=0, has_side_effects=True, vmem_limit_bytes=63 * 1024 * 1024
        ),
    )(*inputs)
    out = pl.pallas_call(
        place_kernel,
        out_shape=shapes,
        in_specs=[vmem] * len(shapes),
        out_specs=[hbm] * len(shapes),
        scratch_shapes=[pltpu.SemaphoreType.DMA((len(shapes),))],
    )(*(pltpu.with_memory_space_constraint(value, pltpu.VMEM) for value in results))
    picture = out[0].transpose(1, 0, 2)[None, None]
    return (picture, out[1], out[2], out[3], out[4].reshape(-1), out[5])


def solution(mesh):
    split = P(None, ("img", "view"))
    placed = (
        split,
        split,
        split,
        P(("img", "view")),
        split,
        P(),
        P("view", "img", None, None),
        P("view", "img", None),
        P("view", "img", None),
        P("view", "img", None, None),
        P("view", "img", None, None, None),
    )
    return jax.shard_map(
        per_device,
        mesh=mesh,
        in_specs=placed,
        out_specs=(P("view", "img", None, None, None), split, split, split, P(("img", "view")), split),
        check_vma=False,
    )
```
